128 devices in a mesh: tm: 32 (over y, x, core), sensor: 4 (over z).
Axes of the slice: x: 4, y: 4, z: 4, core: 2. Of those that a mesh axis runs over, the one named last changes fastest.
Arguments:
- observation_operator: bfloat16 [32768, 128, 128], P(('tm', 'sensor')), may hold values from -0.1875 to 0.1875
- observed_values: bfloat16 [32768, 128], P(('tm', 'sensor')), may hold values from -6 to 6
- observation_weight: float32 [32768, 128], P(('tm', 'sensor')), may hold values from 0.1 to 1
- tile_time_step: int32 [32768], P(('tm', 'sensor')), may hold values from 0 to 127
- tile_state_block: int32 [32768], P(('tm', 'sensor')), may hold values from 0 to 3
- tile_live_count: int32 [32768], P(('tm', 'sensor')), may hold values from 1 to 128
- transition: float32 [512, 512], replicated, may hold values from -1 to 1, as said below
- predicted_precision: float32 [512], replicated, may hold values from 1 to 1000
- starting_mean: float32 [512], replicated, may hold values from -6 to 6
Outputs:
- filtered: float32 [128, 512], P('tm')
- smoothed: float32 [128, 512], P('tm')
The draws below stay inside these ranges and needn't reach their ends.
Inputs may be any that keep to these rules, and one draw needn't show every extreme that they name: `transition`: a dense real matrix.
All inputs are finite; a program needn't handle non-finite values.
Results may differ from the reference program's by a relative error of at most 0.0045.
Values sent between devices are 32-bit elements; how exact they have to be, the bound alone decides.
A program may use at most 128 MiB of HBM per device.

```python
import math
import jax
import jax.numpy as jnp
import numpy as np
from jax import lax

CHAOS_TERMS = 512
TILE = 128
TILES_DEV = 256
NB = 4
TIME = 128
TILES = 32768


def draw_transition(key, part):
    key = jax.random.fold_in(key, 5)
    base = jax.random.normal(key, (CHAOS_TERMS, CHAOS_TERMS), jnp.float32)
    antisym = (base - base.T) * (0.13 / math.sqrt(CHAOS_TERMS))
    return antisym + 0.93 * jnp.eye(CHAOS_TERMS, dtype=jnp.float32)


def with_ends(result, rng, low, high):
    dims = result.shape
    place = [jax.random.randint(jax.random.fold_in(rng, axis), (), 0, dims[axis]) for axis in range(len(dims))]
    result = result.at[tuple(place)].set(low)
    longest = dims.index(max(dims))
    place[longest] = (place[longest] + 1) % dims[longest]
    return result.at[tuple(place)].set(high)


def level_of(rng, extent, cuts, low, top_value):
    def one(axis_at, blocks):
        steps = jax.random.uniform(jax.random.fold_in(jax.random.fold_in(rng, 6), axis_at), (blocks,), jnp.float32, low / len(cuts), top_value / len(cuts))
        return jnp.repeat(jnp.exp(steps), extent[axis_at] // blocks).reshape((-1,) + (1,) * (len(extent) - axis_at - 1))

    gain = one(*cuts[0])
    for cut in cuts[1:]:
        gain = gain * one(*cut)
    return gain


def cumulative_ranks(count, slope):
    loads = [(1 << 20) // math.isqrt(standing ** slope) + 1 for standing in range(1, count + 1)]
    deviation = 1 + sum(loads) // (1 << 30)
    return np.cumsum(np.array([max(1, weight // deviation) for weight in loads]))


def ranked_ids(stream_key, dims, number_of, skew):
    grid = cumulative_ranks(number_of, skew)
    lot = jax.random.randint(jax.random.fold_in(stream_key, 1), dims, 0, int(grid[number_of - 1]))
    standing = jnp.searchsorted(jnp.asarray(grid, jnp.int32), lot, side="right")
    return jax.random.permutation(jax.random.fold_in(stream_key, 2), number_of)[standing].astype(jnp.int32)


def centred(key, shape, deviation, reach, shards=(), held_as=jnp.bfloat16):
    values = jax.random.normal(key, shape, jnp.float32) * deviation
    if len(shards) > 0:
        values = level_of(key, shape, shards, -0.22, 0.18) * values
    return jnp.clip(values, min=-reach, max=reach).astype(held_as)


def setup_inputs(seed: int = 0) -> dict:
    key_of = jax.random.split(jax.random.key(seed), 10)
    return {
        "observation_operator": centred(key_of[0], (TILES, TILE, TILE), (8 * TILE) ** -0.5, 0.1875, ((0, 128),)),
        "observed_values": centred(key_of[1], (TILES, TILE), 1.0, 6.0, ((0, 128),)),
        "observation_weight": jnp.clip(jnp.exp(math.log(1.0) - 2.3025851 * jax.random.uniform(key_of[2], (TILES, TILE), jnp.float32) ** level_of(key_of[2], (TILES, TILE), ((0, 128),), -0.2, 0.2)), 0.1, 1.0),
        "tile_time_step": with_ends(ranked_ids(key_of[3], (TILES,), TIME, 2), jax.random.fold_in(key_of[3], 3), 0, TIME - 1).astype(jnp.int32),
        "tile_state_block": with_ends(jax.random.randint(key_of[4], (TILES,), 0, NB), jax.random.fold_in(key_of[4], 1), 0, NB - 1).astype(jnp.int32),
        "tile_live_count": with_ends(jax.random.randint(key_of[5], (TILES,), 1, TILE + 1), jax.random.fold_in(key_of[5], 1), 1, TILE).astype(jnp.int32),
        "transition": draw_transition(jax.random.fold_in(key_of[9], 71), 0),
        "predicted_precision": jnp.clip(jnp.exp(jax.random.uniform(key_of[7], (CHAOS_TERMS,), jnp.float32, math.log(1.0), math.log(1000.0))), 1.0, 1000.0),
        "starting_mean": centred(key_of[8], (CHAOS_TERMS,), 1.0, 6.0, (), jnp.float32),
    }


top_precision = lax.Precision.HIGHEST


def tile_terms(matrices, values, weights, counts):
    positions = lax.broadcasted_iota(jnp.int32, values.shape, 1)
    live_weight = jnp.where(positions < counts[:, None], weights, 0.0)
    weighted = (live_weight * values.astype(jnp.float32)).astype(jnp.bfloat16)
    wide = matrices.astype(jnp.float32)
    tile_info = jnp.einsum("tko,tk->to", wide, weighted.astype(jnp.float32), precision=top_precision)
    tile_curv = jnp.einsum("tko,tk->to", wide * wide, live_weight, precision=top_precision)
    return tile_info, tile_curv


def reference(observation_operator, observed_values, observation_weight, tile_time_step, tile_state_block, tile_live_count, transition, predicted_precision, starting_mean):
    groups = observation_operator.shape[0] // TILES_DEV
    grouped = (observation_operator.reshape(groups, TILES_DEV, TILE, TILE),
               observed_values.reshape(groups, TILES_DEV, TILE),
               observation_weight.reshape(groups, TILES_DEV, TILE),
               tile_live_count.reshape(groups, TILES_DEV))
    tile_info, tile_curv = lax.map(lambda items: tile_terms(*items), grouped)
    tile_info = tile_info.reshape(-1, TILE)
    tile_curv = tile_curv.reshape(-1, TILE)
    segment_ids = (tile_time_step * NB + tile_state_block).astype(jnp.int32)
    information = jax.ops.segment_sum(tile_info, segment_ids, TIME * NB).reshape(TIME, CHAOS_TERMS)
    observed_flag = jax.ops.segment_sum(tile_curv, segment_ids, TIME * NB).reshape(TIME, CHAOS_TERMS)
    precision_row_list = predicted_precision[None, :] + observed_flag
    kalman_gain_rows = predicted_precision[None, :] / precision_row_list
    drive_rows = information / precision_row_list

    def advance(mean_vec, inputs):
        gain_row, drive_row = inputs
        mean_vec = gain_row * jnp.dot(transition, mean_vec, precision=top_precision) + drive_row
        return mean_vec, mean_vec

    _, filtered = lax.scan(advance, starting_mean, (kalman_gain_rows, drive_rows))
    final_row = lax.broadcasted_iota(jnp.int32, (TIME, 1), 0) == TIME - 1
    smooth_gain = jnp.where(final_row, 0.0, kalman_gain_rows)
    transposed = transition.T

    def retreat(later_vec, inputs):
        gain_row, mean_vec = inputs
        pushed = jnp.dot(transposed, jnp.dot(transition, mean_vec, precision=top_precision), precision=top_precision)
        offset = mean_vec - gain_row * pushed
        value = gain_row * jnp.dot(transposed, later_vec, precision=top_precision) + offset
        return value, value

    _, smoothed = lax.scan(retreat, jnp.zeros((CHAOS_TERMS,), jnp.float32), (smooth_gain, filtered), reverse=True)
    return filtered, smoothed
```

```python
import functools

import jax
import jax.numpy as jnp
from jax import lax
from jax.experimental import pallas as pl
from jax.experimental.pallas import tpu as pltpu
from jax.sharding import PartitionSpec as P

MESH = pl.DeviceIdType.MESH
TILE = 128
GROUPS = (("c",), ("x", "y", "z"))
SIZES = {"c": 2, "x": 4, "y": 4, "z": 4}
F32, BF16 = jnp.float32, jnp.bfloat16


def parts(value):
    upper = value.astype(BF16)
    return upper, (value - upper.astype(F32)).astype(BF16)


def tile_kernel(steps, op_ref, val_ref, wgt_ref, step_ref, block_ref, live_ref, out_ref, lhs, info, curv):
    k = pl.program_id(0)
    tiles = wgt_ref.shape[0]

    @pl.when(k == 0)
    def _():
        for half in range(tiles // TILE):
            rows = pl.ds(half * TILE, TILE)
            count = live_ref[:, half * TILE : (half + 1) * TILE].astype(F32)
            count = jnp.transpose(jnp.broadcast_to(count, (TILE, TILE)))
            columns = lax.broadcasted_iota(jnp.int32, (TILE, TILE), 1).astype(F32)
            live = jnp.where(columns < count, wgt_ref[rows, :], 0.0)
            weighted = (live * val_ref[rows, :].astype(F32)).astype(BF16).astype(F32)
            upper = live.astype(BF16).astype(F32)
            lower = live - upper
            for kind, value in enumerate((weighted, upper, lower, jnp.zeros_like(live))):
                lhs[pl.ds(half * TILE // 8, TILE // 8), kind * 8 : (kind + 1) * 8, :] = value.reshape(
                    TILE // 8, 8, TILE
                )

    each = op_ref.shape[0]
    place = lax.broadcasted_iota(jnp.int32, (8, TILE), 0)
    for group in range(each // 8):
        left = lhs[k * (each // 8) + group].astype(BF16)
        info_sum = jnp.zeros((8, TILE), F32)
        curv_sum = jnp.zeros((8, TILE), F32)
        for j in range(8):
            op = op_ref[group * 8 + j]
            both = jnp.concatenate([op, op * op], axis=1)
            got = jnp.dot(left, both, preferred_element_type=F32)
            info_sum = jnp.where(place == j, got[0:8, :TILE], info_sum)
            curv_sum = jnp.where(place == j, got[8:16, TILE:] + got[16:24, TILE:], curv_sum)
        at = pl.ds(pl.multiple_of(k * each + group * 8, 8), 8)
        info[at, :] = info_sum
        curv[at, :] = curv_sum

    @pl.when(k == steps - 1)
    def _():
        segments = out_ref.shape[0] // 2
        ids = step_ref[...] * 4 + block_ref[...]
        targets = lax.broadcasted_iota(jnp.int32, (segments, tiles), 0)
        onehot = jnp.where(targets == ids, 1.0, 0.0).astype(BF16)
        stack = jnp.concatenate(parts(info[...]) + parts(curv[...]), axis=1)
        sums = jnp.dot(onehot, stack, preferred_element_type=F32)
        out_ref[:segments, :] = sums[:, :TILE] + sums[:, TILE : 2 * TILE]
        out_ref[segments:, :] = sums[:, 2 * TILE : 3 * TILE] + sums[:, 3 * TILE :]


def tile_sums(op, val, wgt, step, block, live, segments):
    tiles = op.shape[0]
    steps = 8
    each = tiles // steps

    def whole(*shape):
        return pl.BlockSpec(shape, lambda k: (0,) * len(shape))

    return pl.pallas_call(
        functools.partial(tile_kernel, steps),
        grid=(steps,),
        out_shape=jax.ShapeDtypeStruct((2 * segments, TILE), F32),
        in_specs=[
            pl.BlockSpec((each, TILE, TILE), lambda k: (k, 0, 0)),
            whole(tiles, TILE),
            whole(tiles, TILE),
            whole(1, tiles),
            whole(1, tiles),
            whole(1, tiles),
        ],
        out_specs=whole(2 * segments, TILE),
        scratch_shapes=[
            pltpu.VMEM((tiles // 8, 32, TILE), F32),
            pltpu.VMEM((tiles, TILE), F32),
            pltpu.VMEM((tiles, TILE), F32),
        ],
        compiler_params=pltpu.CompilerParams(vmem_limit_bytes=32 << 20),
    )(op, val, wgt, step.reshape(1, -1), block.reshape(1, -1), live.reshape(1, -1))


def exchange_kernel(in_ref, out_ref, *scratch):
    count = len(GROUPS)
    works, boxes = scratch[:count], scratch[count : 2 * count]
    send_in, recv_in, send_out, recv_out = scratch[2 * count :]
    tm = lax.axis_index("tm")
    mine = {
        "c": lax.rem(tm, 2),
        "x": lax.rem(lax.div(tm, 2), 4),
        "y": lax.div(tm, 8),
        "z": lax.axis_index("sensor"),
    }

    def device_of(at):
        return (at["y"] * 8 + at["x"] * 2 + at["c"], at["z"])

    def member(group, offset):
        at = dict(mine)
        for axis in group:
            at[axis] = lax.rem(mine[axis] + lax.rem(offset, SIZES[axis]), SIZES[axis])
            offset = lax.div(offset, SIZES[axis])
        return at

    def index_in(group, at):
        index, scale = 0, 1
        for axis in group:
            index = index + at[axis] * scale
            scale *= SIZES[axis]
        return index, scale

    barrier = pltpu.get_barrier_semaphore()
    greeted = 0
    for group in GROUPS:
        size = index_in(group, mine)[1]

        def greet(offset, carry, group=group):
            pl.semaphore_signal(
                barrier, inc=1, device_id=device_of(member(group, offset)), device_id_type=MESH
            )
            return carry

        lax.fori_loop(1, size, greet, 0)
        greeted += size - 1
    pl.semaphore_wait(barrier, greeted)

    source = in_ref
    start, starts = 0, []
    for stage, group in enumerate(GROUPS):
        me, size = index_in(group, mine)
        rows = source.shape[0] // size
        box = boxes[stage]

        def give(offset, carry, source=source, group=group, rows=rows, box=box, stage=stage):
            to = member(group, offset)
            index, _ = index_in(group, to)
            pltpu.make_async_remote_copy(
                src_ref=source.at[pl.ds(pl.multiple_of(index * rows, 8), rows)],
                dst_ref=box.at[pl.ds(pl.multiple_of((offset - 1) * rows, 8), rows)],
                send_sem=send_in.at[stage],
                recv_sem=recv_in.at[stage],
                device_id=device_of(to),
                device_id_type=MESH,
            ).start()
            return carry

        lax.fori_loop(1, size, give, 0)
        pltpu.make_async_copy(box, box, recv_in.at[stage]).wait()
        own = source[pl.ds(pl.multiple_of(me * rows, 8), rows), :]
        works[stage][...] = own + jnp.sum(box[...].reshape(size - 1, rows, TILE), axis=0)
        start = start + me * rows
        starts.append(start)
        source = works[stage]

    last = source.shape[0]
    out_ref[pl.ds(pl.multiple_of(start, 8), last), :] = source[...]
    for stage in reversed(range(count)):
        group = GROUPS[stage]
        size = index_in(group, mine)[1]
        rows = works[stage].shape[0]
        piece = out_ref.at[pl.ds(pl.multiple_of(starts[stage], 8), rows)]

        def spread(offset, carry, group=group, piece=piece, stage=stage):
            pltpu.make_async_remote_copy(
                src_ref=piece,
                dst_ref=piece,
                send_sem=send_out.at[stage],
                recv_sem=recv_out.at[stage],
                device_id=device_of(member(group, offset)),
                device_id_type=MESH,
            ).start()
            return carry

        lax.fori_loop(1, size, spread, 0)
        pltpu.make_async_copy(boxes[stage], boxes[stage], recv_out.at[stage]).wait()
    for stage in range(count):
        pltpu.make_async_copy(boxes[stage], boxes[stage], send_in.at[stage]).wait()
        pltpu.make_async_copy(boxes[stage], boxes[stage], send_out.at[stage]).wait()


def exchange(sums):
    rows, works, boxes = sums.shape[0], [], []
    for group in GROUPS:
        size = 1
        for axis in group:
            size *= SIZES[axis]
        rows //= size
        works.append(pltpu.VMEM((rows, TILE), F32))
        boxes.append(pltpu.VMEM(((size - 1) * rows, TILE), F32))
    return pl.pallas_call(
        exchange_kernel,
        out_shape=jax.ShapeDtypeStruct(sums.shape, F32),
        in_specs=[pl.BlockSpec(memory_space=pltpu.VMEM)],
        out_specs=pl.BlockSpec(memory_space=pltpu.VMEM),
        scratch_shapes=works + boxes + [pltpu.SemaphoreType.DMA((len(GROUPS),))] * 4,
        compiler_params=pltpu.CompilerParams(
            collective_id=0, has_side_effects=True, vmem_limit_bytes=16 << 20
        ),
    )(sums)


def recurrence_kernel(
    sums_ref, tran_ref, flip_ref, prec_ref, start_ref, filt_ref, smooth_ref,
    gain, drive, split, gain_col, diff_col, diff_row, filt_col, extra_row, extra_col, filt_row,
):
    segments = sums_ref.shape[0] // 2
    times = segments // 4
    width = tran_ref.shape[0]
    first = lax.axis_index("tm") * 2

    pp = prec_ref[...]
    pp = jnp.concatenate([pp, pp], axis=0)[None]
    observed = sums_ref[segments:, :].reshape(segments // 8, 8, TILE)
    precision = pp + observed
    inverse = 1.0 / precision
    gain[...] = (pp * inverse).reshape(segments, TILE)
    drive[...] = (sums_ref[:segments, :].reshape(segments // 8, 8, TILE) * inverse).reshape(segments, TILE)
    for kind, ref in enumerate((gain, drive)):
        for b in range(4):
            turned = jnp.transpose(ref[pl.ds(b, times, 4), :])
            upper, lower = parts(turned)
            rows = pl.ds(kind * width + b * TILE, TILE)
            split[rows, :TILE] = upper
            split[rows, TILE:] = lower

    lanes = lax.rem(lax.broadcasted_iota(jnp.int32, (2 * TILE, TILE), 0), TILE)

    def row_to_col(ref, row):
        total = ref[:, :TILE] * row[0]
        for b in range(1, 4):
            total += ref[:, b * TILE : (b + 1) * TILE] * row[b]
        return jnp.sum(total, axis=1, keepdims=True)

    def col_to_row(ref, col):
        return tuple(
            jnp.sum(ref[:, b * TILE : (b + 1) * TILE] * col, axis=0, keepdims=True) for b in range(4)
        )

    def forward(keep, i, row):
        even, odd = 2 * i, 2 * i + 1
        pick = jnp.where(lanes == even, 1.0, 0.0).astype(BF16)
        spread = jnp.dot(split[...], pick, preferred_element_type=F32)
        g_col = spread[:width]
        pushed = row_to_col(tran_ref, row)
        col = g_col * pushed + spread[width:]
        gain_col[i] = g_col
        diff_col[i] = col - pushed
        moved = col_to_row(flip_ref, col)
        out = []
        for b in range(4):
            at = pl.ds(4 * odd + b, 1)
            value = gain[at, :] * moved[b] + drive[at, :]
            diff_row[at, :] = value - moved[b]
            out.append(value)
            if keep is not None:
                filt_row[pl.ds(keep * 4 + b, 1), :] = value
        if keep is not None:
            filt_col[keep] = col
        return tuple(out)

    row = tuple(start_ref[b : b + 1, :] for b in range(4))
    plain = functools.partial(forward, None)
    row = lax.fori_loop(0, first, plain, row)
    row = forward(0, first, row)
    row = forward(1, first + 1, row)
    row = lax.fori_loop(first + 2, times // 2, plain, row)

    ahead = -jnp.broadcast_to(row_to_col(tran_ref, row), (width, TILE))
    gain[4 * (times - 1) :, :] = jnp.zeros((4, TILE), F32)

    def backward(keep, n, ahead):
        i = times // 2 - 1 - n
        odd = 2 * i + 1
        moved = col_to_row(tran_ref, ahead)
        back = []
        for b in range(4):
            at = pl.ds(4 * odd + b, 1)
            value = gain[at, :] * moved[b]
            back.append(value + diff_row[at, :])
            if keep is not None:
                extra_row[pl.ds(keep * 4 + b, 1), :] = value
        col = gain_col[i] * row_to_col(flip_ref, back)
        if keep is not None:
            extra_col[keep] = col
        return col + diff_col[i]

    plain = functools.partial(backward, None)
    half = times // 2
    ahead = lax.fori_loop(0, half - 2 - first, plain, ahead)
    ahead = backward(1, half - 2 - first, ahead)
    ahead = backward(0, half - 1 - first, ahead)
    lax.fori_loop(half - first, half, plain, ahead)

    eye = lax.broadcasted_iota(jnp.int32, (TILE, TILE), 0) == lax.broadcasted_iota(jnp.int32, (TILE, TILE), 1)
    for keep in range(2):
        for b in range(4):
            rows, lane = slice(b * TILE, (b + 1) * TILE), slice(b * TILE, (b + 1) * TILE)
            f = jnp.sum(jnp.where(eye, filt_col[keep, rows, :], 0.0), axis=0, keepdims=True)
            e = jnp.sum(jnp.where(eye, extra_col[keep, rows, :], 0.0), axis=0, keepdims=True)
            filt_ref[2 * keep : 2 * keep + 1, lane] = f
            smooth_ref[2 * keep : 2 * keep + 1, lane] = f + e
            f = filt_row[keep * 4 + b : keep * 4 + b + 1, :]
            filt_ref[2 * keep + 1 : 2 * keep + 2, lane] = f
            smooth_ref[2 * keep + 1 : 2 * keep + 2, lane] = f + extra_row[keep * 4 + b : keep * 4 + b + 1, :]


def recurrence(sums, transition, predicted_precision, starting_mean):
    segments = sums.shape[0] // 2
    width = transition.shape[0]
    times = segments // 4
    vmem = pl.BlockSpec(memory_space=pltpu.VMEM)
    shape = jax.ShapeDtypeStruct((4, width), F32)
    return pl.pallas_call(
        recurrence_kernel,
        out_shape=(shape, shape),
        in_specs=[vmem] * 5,
        out_specs=(vmem, vmem),
        scratch_shapes=[
            pltpu.VMEM((segments, TILE), F32),
            pltpu.VMEM((segments, TILE), F32),
            pltpu.VMEM((2 * width, 2 * TILE), BF16),
            pltpu.VMEM((times // 2, width, TILE), F32),
            pltpu.VMEM((times // 2, width, TILE), F32),
            pltpu.VMEM((segments, TILE), F32),
            pltpu.VMEM((2, width, TILE), F32),
            pltpu.VMEM((8, TILE), F32),
            pltpu.VMEM((2, width, TILE), F32),
            pltpu.VMEM((8, TILE), F32),
        ],
        compiler_params=pltpu.CompilerParams(vmem_limit_bytes=48 << 20),
    )(
        sums,
        transition,
        transition.T,
        predicted_precision.reshape(4, TILE),
        starting_mean.reshape(4, TILE),
    )


def shards(op, val, wgt, step, block, live, transition, predicted_precision, starting_mean):
    segments = 4 * 4 * lax.axis_size("tm")
    sums = tile_sums(op, val, wgt, step, block, live, segments)
    sums = exchange(sums)
    return recurrence(sums, transition, predicted_precision, starting_mean)


def solution(mesh):
    both = ("tm", "sensor")
    in_specs = (P(both, None, None), P(both, None), P(both, None), P(both), P(both), P(both), P(), P(), P())
    out_specs = (P("tm", None), P("tm", None))
    return jax.shard_map(shards, mesh=mesh, in_specs=in_specs, out_specs=out_specs, check_vma=False)
```

```python
import functools

import jax
import jax.numpy as jnp
from jax import lax
from jax.experimental import pallas as pl
from jax.experimental.pallas import tpu as pltpu
from jax.sharding import PartitionSpec as P

MESH = pl.DeviceIdType.MESH
TILE = 128
GROUPS = (("c",), ("x", "y", "z"))
SIZES = {"c": 2, "x": 4, "y": 4, "z": 4}
CHUNK = 128
VMEM = 60 << 20
F32, BF16 = jnp.float32, jnp.bfloat16


def parts(value):
    upper = value.astype(BF16)
    return upper, (value - upper.astype(F32)).astype(BF16)


def coordinates():
    tm = lax.axis_index("tm")
    return {
        "c": lax.rem(tm, 2),
        "x": lax.rem(lax.div(tm, 2), 4),
        "y": lax.div(tm, 8),
        "z": lax.axis_index("sensor"),
    }


def device_of(at):
    return (at["y"] * 8 + at["x"] * 2 + at["c"], at["z"])


def size_of(group):
    size = 1
    for axis in group:
        size *= SIZES[axis]
    return size


def member(mine, group, offset):
    at = dict(mine)
    for axis in group:
        at[axis] = lax.rem(mine[axis] + lax.rem(offset, SIZES[axis]), SIZES[axis])
        offset = lax.div(offset, SIZES[axis])
    return at


def index_in(group, at):
    index, scale = 0, 1
    for axis in group:
        index = index + at[axis] * scale
        scale *= SIZES[axis]
    return index


def greet_all(mine):
    barrier = pltpu.get_barrier_semaphore()
    for group in GROUPS:

        def greet(offset, carry, group=group):
            to = device_of(member(mine, group, offset))
            pl.semaphore_signal(barrier, inc=1, device_id=to, device_id_type=MESH)
            return carry

        lax.fori_loop(1, size_of(group), greet, 0)


def wait_all():
    pl.semaphore_wait(pltpu.get_barrier_semaphore(), sum(size_of(group) - 1 for group in GROUPS))


def exchange(mine, source, out_ref, works, boxes, send_in, recv_in, send_out, recv_out):
    count = len(GROUPS)
    start, starts = 0, []
    for stage, group in enumerate(GROUPS):
        size = size_of(group)
        rows = source.shape[0] // size
        box = boxes[stage]

        def give(offset, carry, source=source, group=group, rows=rows, box=box, stage=stage):
            to = member(mine, group, offset)
            pltpu.make_async_remote_copy(
                src_ref=source.at[pl.ds(pl.multiple_of(index_in(group, to) * rows, 8), rows)],
                dst_ref=box.at[pl.ds(pl.multiple_of((offset - 1) * rows, 8), rows)],
                send_sem=send_in.at[stage],
                recv_sem=recv_in.at[stage],
                device_id=device_of(to),
                device_id_type=MESH,
            ).start()
            return carry

        lax.fori_loop(1, size, give, 0)
        pltpu.make_async_copy(box, box, recv_in.at[stage]).wait()
        me = index_in(group, mine) * rows
        own = source[pl.ds(pl.multiple_of(me, 8), rows), :]
        works[stage][...] = own + jnp.sum(box[...].reshape(size - 1, rows, TILE), axis=0)
        start = start + me
        starts.append(start)
        source = works[stage]

    last = source.shape[0]
    out_ref[pl.ds(pl.multiple_of(start, 8), last), :] = source[...]
    for stage in reversed(range(count)):
        group = GROUPS[stage]
        rows = works[stage].shape[0]
        piece = out_ref.at[pl.ds(pl.multiple_of(starts[stage], 8), rows)]

        def spread(offset, carry, group=group, piece=piece, stage=stage):
            pltpu.make_async_remote_copy(
                src_ref=piece,
                dst_ref=piece,
                send_sem=send_out.at[stage],
                recv_sem=recv_out.at[stage],
                device_id=device_of(member(mine, group, offset)),
                device_id_type=MESH,
            ).start()
            return carry

        lax.fori_loop(1, size_of(group), spread, 0)
        pltpu.make_async_copy(boxes[stage], boxes[stage], recv_out.at[stage]).wait()
    for stage in range(count):
        pltpu.make_async_copy(boxes[stage], boxes[stage], send_in.at[stage]).wait()
        pltpu.make_async_copy(boxes[stage], boxes[stage], send_out.at[stage]).wait()


def tile_kernel(
    steps, op_ref, val_ref, wgt_ref, step_ref, block_ref, live_ref, out_ref, lhs, info, curv, local, all_sums, *scratch
):
    count = len(GROUPS)
    k = pl.program_id(0)
    tiles = wgt_ref.shape[0]
    mine = coordinates()

    @pl.when(k == 0)
    def _():
        greet_all(mine)
        for half in range(tiles // TILE):
            rows = pl.ds(half * TILE, TILE)
            live_count = live_ref[:, half * TILE : (half + 1) * TILE].astype(F32)
            live_count = jnp.transpose(jnp.broadcast_to(live_count, (TILE, TILE)))
            columns = lax.broadcasted_iota(jnp.int32, (TILE, TILE), 1).astype(F32)
            live = jnp.where(columns < live_count, wgt_ref[rows, :], 0.0)
            weighted = (live * val_ref[rows, :].astype(F32)).astype(BF16).astype(F32)
            upper = live.astype(BF16).astype(F32)
            lower = live - upper
            for kind, value in enumerate((weighted, upper, lower, jnp.zeros_like(live))):
                lhs[pl.ds(half * TILE // 8, TILE // 8), kind * 8 : (kind + 1) * 8, :] = value.reshape(
                    TILE // 8, 8, TILE
                )

    each = op_ref.shape[0]
    place = lax.broadcasted_iota(jnp.int32, (8, TILE), 0)
    for group in range(each // 8):
        left = lhs[k * (each // 8) + group].astype(BF16)
        info_sum = jnp.zeros((8, TILE), F32)
        curv_sum = jnp.zeros((8, TILE), F32)
        for j in range(8):
            op = op_ref[group * 8 + j]
            both = jnp.concatenate([op, op * op], axis=1)
            got = jnp.dot(left, both, preferred_element_type=F32)
            info_sum = jnp.where(place == j, got[0:8, :TILE], info_sum)
            curv_sum = jnp.where(place == j, got[8:16, TILE:] + got[16:24, TILE:], curv_sum)
        at = pl.ds(pl.multiple_of(k * each + group * 8, 8), 8)
        info[at, :] = info_sum
        curv[at, :] = curv_sum

    @pl.when(k == steps - 1)
    def _():
        segments = out_ref.shape[0] // 2
        ids = step_ref[...] * 4 + block_ref[...]
        targets = lax.broadcasted_iota(jnp.int32, (segments, tiles), 0)
        onehot = jnp.where(targets == ids, 1.0, 0.0).astype(BF16)
        stack = jnp.concatenate(parts(info[...]) + parts(curv[...]), axis=1)
        sums = jnp.dot(onehot, stack, preferred_element_type=F32)
        local[:segments, :] = sums[:, :TILE] + sums[:, TILE : 2 * TILE]
        local[segments:, :] = sums[:, 2 * TILE : 3 * TILE] + sums[:, 3 * TILE :]
        wait_all()
        exchange(mine, local, all_sums, scratch[:count], scratch[count : 2 * count], *scratch[2 * count :])
        out_ref[...] = all_sums[...]


def summed(op, val, wgt, step, block, live, segments):
    tiles = op.shape[0]
    steps = 8
    each = tiles // steps
    rows, works, boxes = 2 * segments, [], []
    for group in GROUPS:
        size = size_of(group)
        rows //= size
        works.append(pltpu.VMEM((rows, TILE), F32))
        boxes.append(pltpu.VMEM(((size - 1) * rows, TILE), F32))

    def whole(*shape):
        return pl.BlockSpec(shape, lambda k: (0,) * len(shape))

    return pl.pallas_call(
        functools.partial(tile_kernel, steps),
        grid=(steps,),
        out_shape=jax.ShapeDtypeStruct((2 * segments, TILE), F32),
        in_specs=[
            pl.BlockSpec((each, TILE, TILE), lambda k: (k, 0, 0)),
            whole(tiles, TILE),
            whole(tiles, TILE),
            whole(1, tiles),
            whole(1, tiles),
            whole(1, tiles),
        ],
        out_specs=whole(2 * segments, TILE),
        scratch_shapes=[
            pltpu.VMEM((tiles // 8, 32, TILE), F32),
            pltpu.VMEM((tiles, TILE), F32),
            pltpu.VMEM((tiles, TILE), F32),
            pltpu.VMEM((2 * segments, TILE), F32),
            pltpu.VMEM((2 * segments, TILE), F32),
            *works,
            *boxes,
        ]
        + [pltpu.SemaphoreType.DMA((len(GROUPS),))] * 4,
        compiler_params=pltpu.CompilerParams(
            collective_id=0, has_side_effects=True, vmem_limit_bytes=VMEM
        ),
    )(op, val, wgt, step.reshape(1, -1), block.reshape(1, -1), live.reshape(1, -1))


def recurrence_kernel(
    sums_ref, tran_ref, flip_ref, prec_ref, start_ref, filt_ref, smooth_ref,
    gain, drive, drive_on, drive_back, gain_col, diff_col, diff_row, filt_row, extra_row, filt_col, extra_col,
):
    segments = sums_ref.shape[0] // 2
    times = segments // 4
    half = times // 2
    width = tran_ref.shape[0]
    chunks = width // CHUNK
    first = lax.axis_index("tm") * 2

    pp = prec_ref[...]
    pp = jnp.concatenate([pp, pp], axis=0)[None]
    observed = sums_ref[segments:, :].reshape(segments // 8, 8, TILE)
    inform = sums_ref[:segments, :].reshape(segments // 8, 8, TILE)
    inverse = 1.0 / (pp + observed)
    gain[...] = (pp * inverse).reshape(segments, TILE)
    drive[...] = (inform * inverse).reshape(segments, TILE)
    for b in range(4):
        rows = slice(b * TILE, (b + 1) * TILE)
        g = jnp.transpose(gain[pl.ds(b, times, 4), :])
        for i in range(half):
            gain_col[i, rows, :] = jnp.broadcast_to(g[:, 2 * i : 2 * i + 1], (TILE, TILE))

    even_drive = jnp.concatenate([drive[pl.ds(b, half, 8), :] for b in range(4)], axis=1)
    upper, lower = parts(even_drive)
    both = jnp.concatenate([upper, lower], axis=0)
    for ref, moved in ((flip_ref, drive_on), (tran_ref, drive_back)):
        high, low = parts(ref[...])
        main = jnp.dot(both, high, preferred_element_type=F32)
        total = main[:half] + (main[half:] + jnp.dot(upper, low, preferred_element_type=F32))
        for b in range(4):
            moved[b] = total[:, b * TILE : (b + 1) * TILE]

    def part(ref, c, *lead):
        return ref[(*lead, slice(c * CHUNK, (c + 1) * CHUNK), slice(None))].reshape(CHUNK // 8, 8, TILE)

    def block(ref, c, b):
        return ref[c * CHUNK : (c + 1) * CHUNK, b * TILE : (b + 1) * TILE].reshape(CHUNK // 8, 8, TILE)

    def row_to_col(ref, wide, c):
        total = block(ref, c, 0) * wide[0]
        for b in range(1, 4):
            total += block(ref, c, b) * wide[b]
        return jnp.sum(total, axis=2, keepdims=True)

    def gather(ref, col, c, sums):
        for b in range(4):
            sums[b].append(jnp.sum(block(ref, c, b) * col, axis=0))

    def finish(pieces):
        while len(pieces) > 1:
            pieces = [sum(pieces[k : k + 2]) for k in range(0, len(pieces), 2)]
        return jnp.sum(pieces[0], axis=0, keepdims=True)

    def spread(row):
        return [jnp.broadcast_to(r, (8, TILE))[None] for r in row]

    def forward(keep, i, row):
        even, odd = 2 * i, 2 * i + 1
        wide = spread(row)
        sums = [[] for _ in range(4)]
        for c in range(chunks):
            rows = slice(c * CHUNK, (c + 1) * CHUNK)
            bare = row_to_col(tran_ref, wide, c)
            col = part(gain_col, c, i) * bare
            gather(flip_ref, col, c, sums)
            diff_col[i, rows, :] = (col - bare).reshape(CHUNK, TILE)
            if keep is not None:
                filt_col[keep, rows, :] = col.reshape(CHUNK, TILE)
        out = []
        for b in range(4):
            at = pl.ds(4 * odd + b, 1)
            moved = finish(sums[b]) + drive_on[b, pl.ds(i, 1), :]
            value = gain[at, :] * moved + drive[at, :]
            diff_row[at, :] = value - moved
            filt_row[at, :] = value
            out.append(value)
        return tuple(out)

    row = tuple(start_ref[b : b + 1, :] for b in range(4))
    plain = functools.partial(forward, None)
    row = lax.fori_loop(0, first, plain, row)
    row = forward(0, first, row)
    row = forward(1, first + 1, row)
    row = lax.fori_loop(first + 2, half, plain, row)

    def step_back(odd, sums, moved):
        back = []
        for b in range(4):
            at = pl.ds(4 * odd + b, 1)
            value = gain[at, :] * (finish(sums[b]) + moved[b])
            extra_row[at, :] = value
            back.append(value + diff_row[at, :])
        return tuple(back)

    wide = spread(row)
    sums = [[] for _ in range(4)]
    for c in range(chunks):
        gather(tran_ref, -row_to_col(tran_ref, wide, c), c, sums)
    gain[4 * (times - 1) :, :] = jnp.zeros((4, TILE), F32)
    row = step_back(times - 1, sums, [0.0] * 4)

    def backward(keep, i, row):
        wide = spread(row)
        sums = [[] for _ in range(4)]
        for c in range(chunks):
            col = part(gain_col, c, i) * row_to_col(flip_ref, wide, c)
            if keep is not None:
                extra_col[keep, c * CHUNK : (c + 1) * CHUNK, :] = col.reshape(CHUNK, TILE)
            if keep != 0:
                gather(tran_ref, col + part(diff_col, c, i), c, sums)
        if keep == 0:
            return row
        moved = [drive_back[b, pl.ds(i, 1), :] for b in range(4)]
        return step_back(2 * i - 1, sums, moved)

    row = lax.fori_loop(0, half - 2 - first, lambda n, r: backward(None, half - 1 - n, r), row)
    row = backward(1, first + 1, row)
    backward(0, first, row)

    eye = lax.broadcasted_iota(jnp.int32, (TILE, TILE), 0) == lax.broadcasted_iota(jnp.int32, (TILE, TILE), 1)
    for keep in range(2):
        for b in range(4):
            lane = slice(b * TILE, (b + 1) * TILE)
            f = jnp.sum(jnp.where(eye, filt_col[keep, lane, :], 0.0), axis=0, keepdims=True)
            f = f + drive[pl.ds(8 * (first + keep) + b, 1), :]
            e = jnp.sum(jnp.where(eye, extra_col[keep, lane, :], 0.0), axis=0, keepdims=True)
            filt_ref[2 * keep : 2 * keep + 1, lane] = f
            smooth_ref[2 * keep : 2 * keep + 1, lane] = f + e
            at = pl.ds(4 * (2 * (first + keep) + 1) + b, 1)
            f = filt_row[at, :]
            filt_ref[2 * keep + 1 : 2 * keep + 2, lane] = f
            smooth_ref[2 * keep + 1 : 2 * keep + 2, lane] = f + extra_row[at, :]


def recurrence(sums, transition, predicted_precision, starting_mean):
    segments = sums.shape[0] // 2
    width = transition.shape[0]
    times = segments // 4
    vmem = pl.BlockSpec(memory_space=pltpu.VMEM)
    shape = jax.ShapeDtypeStruct((4, width), F32)
    return pl.pallas_call(
        recurrence_kernel,
        out_shape=(shape, shape),
        in_specs=[vmem] * 5,
        out_specs=(vmem, vmem),
        scratch_shapes=[
            pltpu.VMEM((segments, TILE), F32),
            pltpu.VMEM((segments, TILE), F32),
            pltpu.VMEM((4, times // 2, TILE), F32),
            pltpu.VMEM((4, times // 2, TILE), F32),
            pltpu.VMEM((times // 2, width, TILE), F32),
            pltpu.VMEM((times // 2, width, TILE), F32),
            pltpu.VMEM((segments, TILE), F32),
            pltpu.VMEM((segments, TILE), F32),
            pltpu.VMEM((segments, TILE), F32),
            pltpu.VMEM((2, width, TILE), F32),
            pltpu.VMEM((2, width, TILE), F32),
        ],
        compiler_params=pltpu.CompilerParams(vmem_limit_bytes=48 << 20),
    )(
        sums,
        transition,
        transition.T,
        predicted_precision.reshape(4, TILE),
        starting_mean.reshape(4, TILE),
    )


def shards(op, val, wgt, step, block, live, transition, predicted_precision, starting_mean):
    segments = 4 * 4 * lax.axis_size("tm")
    sums = summed(op, val, wgt, step, block, live, segments)
    return recurrence(sums, transition, predicted_precision, starting_mean)


def solution(mesh):
    both = ("tm", "sensor")
    in_specs = (P(both, None, None), P(both, None), P(both, None), P(both), P(both), P(both), P(), P(), P())
    out_specs = (P("tm", None), P("tm", None))
    return jax.shard_map(shards, mesh=mesh, in_specs=in_specs, out_specs=out_specs, check_vma=False)
```

```python
import functools
import itertools

import jax
import jax.numpy as jnp
from jax import lax
from jax.experimental import pallas as pl
from jax.experimental.pallas import tpu as pltpu
from jax.sharding import PartitionSpec as P

MESH = pl.DeviceIdType.MESH
TILE = 128
GROUPS = (("c",), ("y", "x", "z"))
SIZES = {"c": 2, "x": 4, "y": 4, "z": 4}
CHUNK = 128
PARTS = 8
F32, BF16 = jnp.float32, jnp.bfloat16


def parts(value):
    upper = value.astype(BF16)
    return upper, (value - upper.astype(F32)).astype(BF16)


def coordinates():
    tm = lax.axis_index("tm")
    mine = {
        "c": lax.rem(tm, 2),
        "x": lax.rem(lax.div(tm, 2), 4),
        "y": lax.div(tm, 8),
        "z": lax.axis_index("sensor"),
    }
    return {
        axis: [mine[axis]] + [lax.rem(mine[axis] + k, size) for k in range(1, size)]
        for axis, size in SIZES.items()
    }


def hops(offsets):
    return sum(min(offset, 4 - offset) for offset in offsets)


def team(group):
    every = list(itertools.product(*[range(SIZES[axis]) for axis in group]))[1:]
    return sorted(every, key=hops, reverse=True)


def size_of(group):
    return len(team(group)) + 1


def member(near, group, offsets):
    at = {axis: near[axis][0] for axis in SIZES}
    for axis, offset in zip(group, offsets):
        at[axis] = near[axis][offset]
    return at


def device_of(at):
    return (at["y"] * 8 + at["x"] * 2 + at["c"], at["z"])


def index_in(group, at):
    index = 0
    for axis in group:
        index = index * SIZES[axis] + at[axis]
    return index


def greet_all(near):
    barrier = pltpu.get_barrier_semaphore()
    for group in GROUPS:
        for offsets in team(group):
            to = device_of(member(near, group, offsets))
            pl.semaphore_signal(barrier, inc=1, device_id=to, device_id_type=MESH)


def wait_all():
    pl.semaphore_wait(pltpu.get_barrier_semaphore(), sum(size_of(group) - 1 for group in GROUPS))


def scatter(near, source, stage, rows, box, send, recv):
    group = GROUPS[stage]
    for k, offsets in enumerate(team(group)):
        to = member(near, group, offsets)
        pltpu.make_async_remote_copy(
            src_ref=source.at[pl.ds(pl.multiple_of(index_in(group, to) * rows, 8), rows)],
            dst_ref=box.at[pl.ds(k * rows, rows)],
            send_sem=send.at[stage],
            recv_sem=recv.at[stage],
            device_id=device_of(to),
            device_id_type=MESH,
        ).start()


def spread(near, out_ref, start, stage, rows, send, recv):
    group = GROUPS[stage]
    piece = out_ref.at[pl.ds(pl.multiple_of(start, 8), rows)]
    for offsets in team(group):
        pltpu.make_async_remote_copy(
            src_ref=piece,
            dst_ref=piece,
            send_sem=send.at[stage],
            recv_sem=recv.at[stage],
            device_id=device_of(member(near, group, offsets)),
            device_id_type=MESH,
        ).start()


def wait_bytes(box, sem):
    pltpu.make_async_copy(box, box, sem).wait()


def exchange(near, source, out_ref, works, boxes, send_in, recv_in, send_out, recv_out, meanwhile):
    count = len(GROUPS)
    start, starts = 0, []
    for stage, group in enumerate(GROUPS):
        size = size_of(group)
        rows = source.shape[0] // size
        box = boxes[stage]
        scatter(near, source, stage, rows, box, send_in, recv_in)
        me = pl.multiple_of(index_in(group, {axis: near[axis][0] for axis in SIZES}) * rows, 8)
        if stage == count - 1:
            meanwhile()
        wait_bytes(box, recv_in.at[stage])
        own = source[pl.ds(me, rows), :]
        works[stage][...] = own + jnp.sum(box[...].reshape(size - 1, rows, TILE), axis=0)
        start = start + me
        starts.append(start)
        source = works[stage]

    out_ref[pl.ds(pl.multiple_of(start, 8), source.shape[0]), :] = source[...]
    for stage in reversed(range(count)):
        spread(near, out_ref, starts[stage], stage, works[stage].shape[0], send_out, recv_out)
        wait_bytes(boxes[stage], recv_out.at[stage])
    for stage in range(count):
        wait_bytes(boxes[stage], send_in.at[stage])
        wait_bytes(boxes[stage], send_out.at[stage])


def tile_kernel(
    op_ref, val_hbm, wgt_hbm, step_hbm, block_hbm, live_hbm, tran_hbm, prec_hbm, start_hbm,
    filt_ref, smooth_ref,
    out_ref, tran_ref, flip_ref, prec_ref, start_ref, tiles_ref, val_ref, wgt_ref, step_ref, block_ref, live_ref, lhs, info, curv, local, small_sem, tile_sem,
    *scratch,
):
    count = len(GROUPS)
    scratch, own = scratch[: 2 * count + 4], scratch[2 * count + 4 :]
    tiles = op_ref.shape[0]
    each = tiles // PARTS
    small = ((live_hbm, live_ref), (wgt_hbm, wgt_ref), (val_hbm, val_ref), (step_hbm, step_ref), (block_hbm, block_ref),
             (tran_hbm, tran_ref), (prec_hbm, prec_ref), (start_hbm, start_ref))
    small = [pltpu.make_async_copy(a, b, small_sem.at[k]) for k, (a, b) in enumerate(small)]
    for copy in small[:3]:
        copy.start()

    def load(k):
        at = pl.ds(pl.multiple_of(k * each, each), each)
        return pltpu.make_async_copy(op_ref.at[at], tiles_ref.at[at], tile_sem.at[k])

    for k in range(PARTS):
        load(k).start()
    for copy in small[3:]:
        copy.start()
    near = coordinates()
    greet_all(near)

    for copy in small[:3]:
        copy.wait()
    for half in range(tiles // TILE):
        rows = pl.ds(half * TILE, TILE)
        live_count = live_ref[:, half * TILE : (half + 1) * TILE].astype(F32)
        live_count = jnp.transpose(jnp.broadcast_to(live_count, (TILE, TILE)))
        columns = lax.broadcasted_iota(jnp.int32, (TILE, TILE), 1).astype(F32)
        live = jnp.where(columns < live_count, wgt_ref[rows, :], 0.0)
        weighted = (live * val_ref[rows, :].astype(F32)).astype(BF16).astype(F32)
        upper = live.astype(BF16).astype(F32)
        lower = live - upper
        for kind, value in enumerate((weighted, upper, lower, jnp.zeros_like(live))):
            lhs[pl.ds(half * TILE // 8, TILE // 8), kind * 8 : (kind + 1) * 8, :] = value.reshape(TILE // 8, 8, TILE)

    place = lax.broadcasted_iota(jnp.int32, (8, TILE), 0)

    def part_sums(k, carry):
        load(k).wait()
        for group in range(each // 8):
            left = lhs[k * (each // 8) + group].astype(BF16)
            info_sum = jnp.zeros((8, TILE), F32)
            curv_sum = jnp.zeros((8, TILE), F32)
            for j in range(8):
                op = tiles_ref[k * each + group * 8 + j]
                both = jnp.concatenate([op, op * op], axis=1)
                got = jnp.dot(left, both, preferred_element_type=F32)
                info_sum = jnp.where(place == j, got[0:8, :TILE], info_sum)
                curv_sum = jnp.where(place == j, got[8:16, TILE:] + got[16:24, TILE:], curv_sum)
            at = pl.ds(pl.multiple_of(k * each + group * 8, 8), 8)
            info[at, :] = info_sum
            curv[at, :] = curv_sum
        return carry

    lax.fori_loop(0, PARTS, part_sums, 0)

    for copy in small[3:5]:
        copy.wait()
    segments = out_ref.shape[0] // 2
    ids = step_ref[...] * 4 + block_ref[...]
    targets = lax.broadcasted_iota(jnp.int32, (segments, tiles), 0)
    onehot = jnp.where(targets == ids, 1.0, 0.0).astype(BF16)
    stack = jnp.concatenate(parts(info[...]) + parts(curv[...]), axis=1)
    sums = jnp.dot(onehot, stack, preferred_element_type=F32)
    inform = (sums[:, :TILE] + sums[:, TILE : 2 * TILE]).reshape(segments // 8, 1, 8, TILE)
    observed = (sums[:, 2 * TILE : 3 * TILE] + sums[:, 3 * TILE :]).reshape(segments // 8, 1, 8, TILE)
    local[...] = jnp.concatenate([inform, observed], axis=1).reshape(2 * segments, TILE)
    wait_all()

    def meanwhile():
        for copy in small[5:]:
            copy.wait()
        for i in range(tran_ref.shape[0] // TILE):
            for j in range(tran_ref.shape[0] // TILE):
                a, b = slice(i * TILE, (i + 1) * TILE), slice(j * TILE, (j + 1) * TILE)
                flip_ref[b, a] = jnp.transpose(tran_ref[a, b])

    exchange(near, local, out_ref, scratch[:count], scratch[count : 2 * count], *scratch[2 * count :], meanwhile)
    recurrence(out_ref, tran_ref, flip_ref, prec_ref, start_ref, filt_ref, smooth_ref, *own)


def recurrence(
    sums_ref, tran_ref, flip_ref, prec_ref, start_ref, filt_ref, smooth_ref,
    gain, drive, drive_on, drive_back, gain_col, diff_col, diff_row, filt_row, extra_row, filt_col, extra_col,
):
    segments = sums_ref.shape[0] // 2
    times = segments // 4
    half = times // 2
    width = tran_ref.shape[0]
    chunks = width // CHUNK
    first = lax.axis_index("tm") * 2

    pp = prec_ref[...]
    pp = jnp.concatenate([pp, pp], axis=0)[None]
    both = sums_ref[...].reshape(segments // 8, 2, 8, TILE)
    inform, observed = both[:, 0], both[:, 1]
    inverse = 1.0 / (pp + observed)
    gain[...] = (pp * inverse).reshape(segments, TILE)
    drive[...] = (inform * inverse).reshape(segments, TILE)
    for b in range(4):
        rows = slice(b * TILE, (b + 1) * TILE)
        g = jnp.transpose(gain[pl.ds(b, times, 4), :])
        for i in range(half):
            gain_col[i, rows, :] = jnp.broadcast_to(g[:, 2 * i : 2 * i + 1], (TILE, TILE))

    even_drive = jnp.concatenate([drive[pl.ds(b, half, 8), :] for b in range(4)], axis=1)
    upper, lower = parts(even_drive)
    both = jnp.concatenate([upper, lower], axis=0)
    for ref, moved in ((flip_ref, drive_on), (tran_ref, drive_back)):
        high, low = parts(ref[...])
        main = jnp.dot(both, high, preferred_element_type=F32)
        total = main[:half] + (main[half:] + jnp.dot(upper, low, preferred_element_type=F32))
        for b in range(4):
            moved[b] = total[:, b * TILE : (b + 1) * TILE]

    def part(ref, c, *lead):
        return ref[(*lead, slice(c * CHUNK, (c + 1) * CHUNK), slice(None))].reshape(CHUNK // 8, 8, TILE)

    def block(ref, c, b):
        return ref[c * CHUNK : (c + 1) * CHUNK, b * TILE : (b + 1) * TILE].reshape(CHUNK // 8, 8, TILE)

    def row_to_col(ref, wide, c):
        total = block(ref, c, 0) * wide[0]
        for b in range(1, 4):
            total += block(ref, c, b) * wide[b]
        return jnp.sum(total, axis=2, keepdims=True)

    def gather(ref, col, c, sums):
        for b in range(4):
            sums[b].append(jnp.sum(block(ref, c, b) * col, axis=0))

    def finish(pieces):
        while len(pieces) > 1:
            pieces = [sum(pieces[k : k + 2]) for k in range(0, len(pieces), 2)]
        return jnp.sum(pieces[0], axis=0, keepdims=True)

    def spread(row):
        return [jnp.broadcast_to(r, (8, TILE))[None] for r in row]

    def forward(keep, i, row):
        even, odd = 2 * i, 2 * i + 1
        wide = spread(row)
        sums = [[] for _ in range(4)]
        for c in range(chunks):
            rows = slice(c * CHUNK, (c + 1) * CHUNK)
            bare = row_to_col(tran_ref, wide, c)
            col = part(gain_col, c, i) * bare
            gather(flip_ref, col, c, sums)
            diff_col[i, rows, :] = (col - bare).reshape(CHUNK, TILE)
            if keep is not None:
                filt_col[keep, rows, :] = col.reshape(CHUNK, TILE)
        out = []
        for b in range(4):
            at = pl.ds(4 * odd + b, 1)
            moved = finish(sums[b]) + drive_on[b, pl.ds(i, 1), :]
            value = gain[at, :] * moved + drive[at, :]
            diff_row[at, :] = value - moved
            filt_row[at, :] = value
            out.append(value)
        return tuple(out)

    row = tuple(start_ref[b : b + 1, :] for b in range(4))
    plain = functools.partial(forward, None)
    row = lax.fori_loop(0, first, plain, row)
    row = forward(0, first, row)
    row = forward(1, first + 1, row)
    row = lax.fori_loop(first + 2, half, plain, row)

    def step_back(odd, sums, moved):
        back = []
        for b in range(4):
            at = pl.ds(4 * odd + b, 1)
            value = gain[at, :] * (finish(sums[b]) + moved[b])
            extra_row[at, :] = value
            back.append(value + diff_row[at, :])
        return tuple(back)

    wide = spread(row)
    sums = [[] for _ in range(4)]
    for c in range(chunks):
        gather(tran_ref, -row_to_col(tran_ref, wide, c), c, sums)
    gain[4 * (times - 1) :, :] = jnp.zeros((4, TILE), F32)
    row = step_back(times - 1, sums, [0.0] * 4)

    def backward(keep, i, row):
        wide = spread(row)
        sums = [[] for _ in range(4)]
        for c in range(chunks):
            col = part(gain_col, c, i) * row_to_col(flip_ref, wide, c)
            if keep is not None:
                extra_col[keep, c * CHUNK : (c + 1) * CHUNK, :] = col.reshape(CHUNK, TILE)
            if keep != 0:
                gather(tran_ref, col + part(diff_col, c, i), c, sums)
        if keep == 0:
            return row
        moved = [drive_back[b, pl.ds(i, 1), :] for b in range(4)]
        return step_back(2 * i - 1, sums, moved)

    row = lax.fori_loop(0, half - 2 - first, lambda n, r: backward(None, half - 1 - n, r), row)
    row = backward(1, first + 1, row)
    backward(0, first, row)

    eye = lax.broadcasted_iota(jnp.int32, (TILE, TILE), 0) == lax.broadcasted_iota(jnp.int32, (TILE, TILE), 1)
    for keep in range(2):
        for b in range(4):
            lane = slice(b * TILE, (b + 1) * TILE)
            f = jnp.sum(jnp.where(eye, filt_col[keep, lane, :], 0.0), axis=0, keepdims=True)
            f = f + drive[pl.ds(8 * (first + keep) + b, 1), :]
            e = jnp.sum(jnp.where(eye, extra_col[keep, lane, :], 0.0), axis=0, keepdims=True)
            filt_ref[2 * keep : 2 * keep + 1, lane] = f
            smooth_ref[2 * keep : 2 * keep + 1, lane] = f + e
            at = pl.ds(4 * (2 * (first + keep) + 1) + b, 1)
            f = filt_row[at, :]
            filt_ref[2 * keep + 1 : 2 * keep + 2, lane] = f
            smooth_ref[2 * keep + 1 : 2 * keep + 2, lane] = f + extra_row[at, :]


def smoother(op, val, wgt, step, block, live, transition, predicted_precision, starting_mean, segments):
    tiles = op.shape[0]
    width = transition.shape[0]
    times = segments // 4
    rows, works, boxes = 2 * segments, [], []
    for group in GROUPS:
        size = size_of(group)
        rows //= size
        works.append(pltpu.VMEM((rows, TILE), F32))
        boxes.append(pltpu.VMEM(((size - 1) * rows, TILE), F32))
    hbm, vmem = pl.BlockSpec(memory_space=pltpu.HBM), pl.BlockSpec(memory_space=pltpu.VMEM)
    shape = jax.ShapeDtypeStruct((4, width), F32)
    return pl.pallas_call(
        tile_kernel,
        out_shape=(shape, shape),
        in_specs=[hbm] * 9,
        out_specs=(vmem, vmem),
        scratch_shapes=[
            pltpu.VMEM((2 * segments, TILE), F32),
            pltpu.VMEM((width, width), F32),
            pltpu.VMEM((width, width), F32),
            pltpu.VMEM((4, TILE), F32),
            pltpu.VMEM((4, TILE), F32),
            pltpu.VMEM((tiles, TILE, TILE), BF16),
            pltpu.VMEM((tiles, TILE), BF16),
            pltpu.VMEM((tiles, TILE), F32),
            pltpu.VMEM((1, tiles), jnp.int32),
            pltpu.VMEM((1, tiles), jnp.int32),
            pltpu.VMEM((1, tiles), jnp.int32),
            pltpu.VMEM((tiles // 8, 32, TILE), F32),
            pltpu.VMEM((tiles, TILE), F32),
            pltpu.VMEM((tiles, TILE), F32),
            pltpu.VMEM((2 * segments, TILE), F32),
            pltpu.SemaphoreType.DMA((8,)),
            pltpu.SemaphoreType.DMA((PARTS,)),
            *works,
            *boxes,
            *[pltpu.SemaphoreType.DMA((len(GROUPS),))] * 4,
            pltpu.VMEM((segments, TILE), F32),
            pltpu.VMEM((segments, TILE), F32),
            pltpu.VMEM((4, times // 2, TILE), F32),
            pltpu.VMEM((4, times // 2, TILE), F32),
            pltpu.VMEM((times // 2, width, TILE), F32),
            pltpu.VMEM((times // 2, width, TILE), F32),
            pltpu.VMEM((segments, TILE), F32),
            pltpu.VMEM((segments, TILE), F32),
            pltpu.VMEM((segments, TILE), F32),
            pltpu.VMEM((2, width, TILE), F32),
            pltpu.VMEM((2, width, TILE), F32),
        ],
        compiler_params=pltpu.CompilerParams(
            collective_id=0, has_side_effects=True, vmem_limit_bytes=62 << 20
        ),
    )(
        op,
        val,
        wgt,
        step.reshape(1, -1),
        block.reshape(1, -1),
        live.reshape(1, -1),
        transition,
        predicted_precision.reshape(4, TILE),
        starting_mean.reshape(4, TILE),
    )


def shards(op, val, wgt, step, block, live, transition, predicted_precision, starting_mean):
    segments = 4 * 4 * lax.axis_size("tm")
    return smoother(
        op, val, wgt, step, block, live, transition, predicted_precision, starting_mean, segments
    )


def solution(mesh):
    both = ("tm", "sensor")
    in_specs = (P(both, None, None), P(both, None), P(both, None), P(both), P(both), P(both), P(), P(), P())
    out_specs = (P("tm", None), P("tm", None))
    return jax.shard_map(shards, mesh=mesh, in_specs=in_specs, out_specs=out_specs, check_vma=False)
```

```python
import functools
import itertools

import jax
import jax.numpy as jnp
from jax import lax
from jax.experimental import pallas as pl
from jax.experimental.pallas import tpu as pltpu
from jax.sharding import PartitionSpec as P

MESH = pl.DeviceIdType.MESH
TILE = 128
SIZES = {"c": 2, "x": 4, "y": 4, "z": 4}
CHUNK = 128
PARTS = 8
F32, BF16 = jnp.float32, jnp.bfloat16


def parts(value):
    upper = value.astype(BF16)
    return upper, (value - upper.astype(F32)).astype(BF16)


def coordinates():
    tm = lax.axis_index("tm")
    mine = {
        "c": lax.rem(tm, 2),
        "x": lax.rem(lax.div(tm, 2), 4),
        "y": lax.div(tm, 8),
        "z": lax.axis_index("sensor"),
    }
    return {
        axis: [mine[axis]] + [lax.rem(mine[axis] + k, size) for k in range(1, size)]
        for axis, size in SIZES.items()
    }


def hops(offsets):
    return sum(min(offset, 4 - offset) for offset in offsets)


PLANE = sorted(itertools.product(range(4), range(4)), key=hops, reverse=True)


def device_of(y, x, z, core):
    return (y * 8 + x * 2 + core, z)


def chip_of(y, x, z):
    return (y * 4 + x) * 4 + z


def partners(near):
    core, half = near["c"][0], lax.div(near["y"][0], 2)
    for k, (dx, dz) in enumerate(PLANE):
        for a in range(2):
            yield 2 * core + a, near["x"][dx], near["z"][dz], half, k, (dx, dz) == (0, 0)


def to_partners(near, act, at_home=None):
    for y, x, z, core, k, close in partners(near):
        if close:
            pl.when(y != near["y"][0])(functools.partial(act, y, x, z, core, k))
            if at_home is not None:
                pl.when(y == near["y"][0])(functools.partial(at_home, y, x, z, core, k))
        else:
            act(y, x, z, core, k)


def is_home(near):
    return lax.div(near["y"][0], 2) == near["c"][0]


def wait_bytes(ref, sem):
    pltpu.make_async_copy(ref, ref, sem).wait()


def wait_partners(near, box, sem):
    rows = box.shape[0]
    home = is_home(near)

    @pl.when(home)
    def _():
        wait_bytes(box.at[pl.ds(0, rows - rows // 32)], sem)

    @pl.when(jnp.logical_not(home))
    def _():
        wait_bytes(box, sem)


def greet_all(near):
    barrier = pltpu.get_barrier_semaphore()
    y, x, z = near["y"][0], near["x"][0], near["z"][0]
    pl.semaphore_signal(barrier, inc=1, device_id=device_of(y, x, z, near["c"][1]), device_id_type=MESH)

    def greet(y, x, z, core, k):
        pl.semaphore_signal(barrier, inc=1, device_id=device_of(y, x, z, core), device_id_type=MESH)

    to_partners(near, greet)


def wait_all(near):
    pl.semaphore_wait(pltpu.get_barrier_semaphore(), jnp.where(is_home(near), 32, 33))


def exchange(near, source, out_ref, half_sum, pair_box, box, mine, twin, sems, meanwhile):
    core, y, x, z = near["c"][0], near["y"][0], near["x"][0], near["z"][0]
    sibling = device_of(y, x, z, near["c"][1])
    half_rows = half_sum.shape[0]
    rows = mine.shape[0]
    here = chip_of(y, x, z)

    def to_sibling(src, dst, k):
        copy = pltpu.make_async_remote_copy(
            src_ref=src,
            dst_ref=dst,
            send_sem=sems.at[2 * k],
            recv_sem=sems.at[2 * k + 1],
            device_id=sibling,
            device_id_type=MESH,
        )
        copy.start()
        return copy

    kept = pl.multiple_of(core * half_rows, 8)
    given = pl.multiple_of((1 - core) * half_rows, 8)
    first = to_sibling(source.at[pl.ds(given, half_rows)], pair_box, 0)
    first.wait_recv()
    half_sum[...] = source[pl.ds(kept, half_rows), :] + pair_box[...]

    def slot(k):
        return pl.ds(pl.multiple_of((lax.rem(y, 2) * 16 + k) * rows, 8), rows)

    def give(to_y, to_x, to_z, to_core, k):
        at = pl.multiple_of((chip_of(to_y, to_x, to_z) - 32 * core) * rows, 8)
        pltpu.make_async_remote_copy(
            src_ref=half_sum.at[pl.ds(at, rows)],
            dst_ref=box.at[slot(k)],
            send_sem=sems.at[2],
            recv_sem=sems.at[3],
            device_id=device_of(to_y, to_x, to_z, to_core),
            device_id_type=MESH,
        ).start()

    def keep(to_y, to_x, to_z, to_core, k):
        at = pl.multiple_of((here - 32 * core) * rows, 8)
        box[slot(k), :] = half_sum[pl.ds(at, rows), :]

    to_partners(near, give, keep)
    meanwhile()
    wait_partners(near, box, sems.at[3])
    mine[...] = jnp.sum(box[...].reshape(32, rows, TILE), axis=0)
    second = to_sibling(mine, twin, 2)
    second.wait_recv()
    total = mine[...] + twin[...]
    second.wait_send()
    mine[...] = total
    place = pl.ds(pl.multiple_of(here * rows, 8), rows)

    def spread(to_y, to_x, to_z, to_core, k):
        pltpu.make_async_remote_copy(
            src_ref=mine,
            dst_ref=out_ref.at[place],
            send_sem=sems.at[6],
            recv_sem=sems.at[7],
            device_id=device_of(to_y, to_x, to_z, to_core),
            device_id_type=MESH,
        ).start()

    def keep_sum(to_y, to_x, to_z, to_core, k):
        out_ref[place, :] = total

    to_partners(near, spread, keep_sum)
    wait_partners(near, box, sems.at[7])
    have = out_ref.at[pl.ds(kept, half_rows)]
    third = to_sibling(have, have, 4)
    third.wait_recv()
    wait_partners(near, box, sems.at[2])
    wait_partners(near, box, sems.at[6])
    first.wait_send()
    third.wait_send()


def tile_kernel(
    op_ref, val_hbm, wgt_hbm, step_hbm, block_hbm, live_hbm, tran_hbm, prec_hbm, start_hbm,
    filt_ref, smooth_ref,
    out_ref, tran_ref, flip_ref, prec_ref, start_ref, tiles_ref, val_ref, wgt_ref, step_ref, block_ref, live_ref, lhs, info, curv, local, small_sem, tile_sem,
    *scratch,
):
    scratch, own = scratch[:6], scratch[6:]
    tiles = op_ref.shape[0]
    each = tiles // PARTS
    small = ((live_hbm, live_ref), (wgt_hbm, wgt_ref), (val_hbm, val_ref), (step_hbm, step_ref), (block_hbm, block_ref),
             (tran_hbm, tran_ref), (prec_hbm, prec_ref), (start_hbm, start_ref))
    small = [pltpu.make_async_copy(a, b, small_sem.at[k]) for k, (a, b) in enumerate(small)]
    for copy in small[:3]:
        copy.start()

    def load(k):
        at = pl.ds(pl.multiple_of(k * each, each), each)
        return pltpu.make_async_copy(op_ref.at[at], tiles_ref.at[at], tile_sem.at[k])

    for k in range(PARTS):
        load(k).start()
    for copy in small[3:]:
        copy.start()
    near = coordinates()
    greet_all(near)

    for copy in small[:3]:
        copy.wait()
    for half in range(tiles // TILE):
        rows = pl.ds(half * TILE, TILE)
        live_count = live_ref[:, half * TILE : (half + 1) * TILE].astype(F32)
        live_count = jnp.transpose(jnp.broadcast_to(live_count, (TILE, TILE)))
        columns = lax.broadcasted_iota(jnp.int32, (TILE, TILE), 1).astype(F32)
        live = jnp.where(columns < live_count, wgt_ref[rows, :], 0.0)
        weighted = (live * val_ref[rows, :].astype(F32)).astype(BF16).astype(F32)
        upper = live.astype(BF16).astype(F32)
        lower = live - upper
        for kind, value in enumerate((weighted, upper, lower, jnp.zeros_like(live))):
            lhs[pl.ds(half * TILE // 8, TILE // 8), kind * 8 : (kind + 1) * 8, :] = value.reshape(TILE // 8, 8, TILE)

    place = lax.broadcasted_iota(jnp.int32, (8, TILE), 0)

    def part_sums(k, carry):
        load(k).wait()
        for group in range(each // 8):
            left = lhs[k * (each // 8) + group].astype(BF16)
            info_sum = jnp.zeros((8, TILE), F32)
            curv_sum = jnp.zeros((8, TILE), F32)
            for j in range(8):
                op = tiles_ref[k * each + group * 8 + j]
                both = jnp.concatenate([op, op * op], axis=1)
                got = jnp.dot(left, both, preferred_element_type=F32)
                info_sum = jnp.where(place == j, got[0:8, :TILE], info_sum)
                curv_sum = jnp.where(place == j, got[8:16, TILE:] + got[16:24, TILE:], curv_sum)
            at = pl.ds(pl.multiple_of(k * each + group * 8, 8), 8)
            info[at, :] = info_sum
            curv[at, :] = curv_sum
        return carry

    lax.fori_loop(0, PARTS, part_sums, 0)

    for copy in small[3:5]:
        copy.wait()
    segments = out_ref.shape[0] // 2
    ids = step_ref[...] * 4 + block_ref[...]
    targets = lax.broadcasted_iota(jnp.int32, (segments, tiles), 0)
    onehot = jnp.where(targets == ids, 1.0, 0.0).astype(BF16)
    stack = jnp.concatenate(parts(info[...]) + parts(curv[...]), axis=1)
    sums = jnp.dot(onehot, stack, preferred_element_type=F32)
    inform = (sums[:, :TILE] + sums[:, TILE : 2 * TILE]).reshape(segments // 8, 1, 8, TILE)
    observed = (sums[:, 2 * TILE : 3 * TILE] + sums[:, 3 * TILE :]).reshape(segments // 8, 1, 8, TILE)
    local[...] = jnp.concatenate([inform, observed], axis=1).reshape(2 * segments, TILE)
    wait_all(near)

    def meanwhile():
        for copy in small[5:]:
            copy.wait()
        for i in range(tran_ref.shape[0] // TILE):
            for j in range(tran_ref.shape[0] // TILE):
                a, b = slice(i * TILE, (i + 1) * TILE), slice(j * TILE, (j + 1) * TILE)
                flip_ref[b, a] = jnp.transpose(tran_ref[a, b])

    exchange(near, local, out_ref, *scratch, meanwhile)
    recurrence(out_ref, tran_ref, flip_ref, prec_ref, start_ref, filt_ref, smooth_ref, *own)


def recurrence(
    sums_ref, tran_ref, flip_ref, prec_ref, start_ref, filt_ref, smooth_ref,
    gain, drive, drive_on, drive_back, gain_col, diff_col, diff_row, filt_row, extra_row, filt_col, extra_col,
):
    segments = sums_ref.shape[0] // 2
    times = segments // 4
    half = times // 2
    width = tran_ref.shape[0]
    chunks = width // CHUNK
    first = lax.axis_index("tm") * 2

    pp = prec_ref[...]
    pp = jnp.concatenate([pp, pp], axis=0)[None]
    both = sums_ref[...].reshape(segments // 8, 2, 8, TILE)
    inform, observed = both[:, 0], both[:, 1]
    inverse = 1.0 / (pp + observed)
    gain[...] = (pp * inverse).reshape(segments, TILE)
    drive[...] = (inform * inverse).reshape(segments, TILE)
    for b in range(4):
        rows = slice(b * TILE, (b + 1) * TILE)
        g = jnp.transpose(gain[pl.ds(b, times, 4), :])
        for i in range(half):
            gain_col[i, rows, :] = jnp.broadcast_to(g[:, 2 * i : 2 * i + 1], (TILE, TILE))

    even_drive = jnp.concatenate([drive[pl.ds(b, half, 8), :] for b in range(4)], axis=1)
    upper, lower = parts(even_drive)
    both = jnp.concatenate([upper, lower], axis=0)
    for ref, moved in ((flip_ref, drive_on), (tran_ref, drive_back)):
        high, low = parts(ref[...])
        main = jnp.dot(both, high, preferred_element_type=F32)
        total = main[:half] + (main[half:] + jnp.dot(upper, low, preferred_element_type=F32))
        for b in range(4):
            moved[b] = total[:, b * TILE : (b + 1) * TILE]

    def part(ref, c, *lead):
        return ref[(*lead, slice(c * CHUNK, (c + 1) * CHUNK), slice(None))].reshape(CHUNK // 8, 8, TILE)

    def block(ref, c, b):
        return ref[c * CHUNK : (c + 1) * CHUNK, b * TILE : (b + 1) * TILE].reshape(CHUNK // 8, 8, TILE)

    def row_to_col(ref, wide, c):
        total = block(ref, c, 0) * wide[0]
        for b in range(1, 4):
            total += block(ref, c, b) * wide[b]
        return jnp.sum(total, axis=2, keepdims=True)

    def gather(ref, col, c, sums):
        for b in range(4):
            sums[b].append(jnp.sum(block(ref, c, b) * col, axis=0))

    def finish(pieces):
        while len(pieces) > 1:
            pieces = [sum(pieces[k : k + 2]) for k in range(0, len(pieces), 2)]
        return jnp.sum(pieces[0], axis=0, keepdims=True)

    def spread(row):
        return [jnp.broadcast_to(r, (8, TILE))[None] for r in row]

    def forward(keep, i, row):
        even, odd = 2 * i, 2 * i + 1
        wide = spread(row)
        sums = [[] for _ in range(4)]
        for c in range(chunks):
            rows = slice(c * CHUNK, (c + 1) * CHUNK)
            bare = row_to_col(tran_ref, wide, c)
            col = part(gain_col, c, i) * bare
            gather(flip_ref, col, c, sums)
            diff_col[i, rows, :] = (col - bare).reshape(CHUNK, TILE)
            if keep is not None:
                filt_col[keep, rows, :] = col.reshape(CHUNK, TILE)
        out = []
        for b in range(4):
            at = pl.ds(4 * odd + b, 1)
            moved = finish(sums[b]) + drive_on[b, pl.ds(i, 1), :]
            value = gain[at, :] * moved + drive[at, :]
            diff_row[at, :] = value - moved
            filt_row[at, :] = value
            out.append(value)
        return tuple(out)

    row = tuple(start_ref[b : b + 1, :] for b in range(4))
    plain = functools.partial(forward, None)
    row = lax.fori_loop(0, first, plain, row)
    row = forward(0, first, row)
    row = forward(1, first + 1, row)
    row = lax.fori_loop(first + 2, half, plain, row)

    def step_back(odd, sums, moved):
        back = []
        for b in range(4):
            at = pl.ds(4 * odd + b, 1)
            value = gain[at, :] * (finish(sums[b]) + moved[b])
            extra_row[at, :] = value
            back.append(value + diff_row[at, :])
        return tuple(back)

    wide = spread(row)
    sums = [[] for _ in range(4)]
    for c in range(chunks):
        gather(tran_ref, -row_to_col(tran_ref, wide, c), c, sums)
    gain[4 * (times - 1) :, :] = jnp.zeros((4, TILE), F32)
    row = step_back(times - 1, sums, [0.0] * 4)

    def backward(keep, i, row):
        wide = spread(row)
        sums = [[] for _ in range(4)]
        for c in range(chunks):
            col = part(gain_col, c, i) * row_to_col(flip_ref, wide, c)
            if keep is not None:
                extra_col[keep, c * CHUNK : (c + 1) * CHUNK, :] = col.reshape(CHUNK, TILE)
            if keep != 0:
                gather(tran_ref, col + part(diff_col, c, i), c, sums)
        if keep == 0:
            return row
        moved = [drive_back[b, pl.ds(i, 1), :] for b in range(4)]
        return step_back(2 * i - 1, sums, moved)

    row = lax.fori_loop(0, half - 2 - first, lambda n, r: backward(None, half - 1 - n, r), row)
    row = backward(1, first + 1, row)
    backward(0, first, row)

    eye = lax.broadcasted_iota(jnp.int32, (TILE, TILE), 0) == lax.broadcasted_iota(jnp.int32, (TILE, TILE), 1)
    for keep in range(2):
        for b in range(4):
            lane = slice(b * TILE, (b + 1) * TILE)
            f = jnp.sum(jnp.where(eye, filt_col[keep, lane, :], 0.0), axis=0, keepdims=True)
            f = f + drive[pl.ds(8 * (first + keep) + b, 1), :]
            e = jnp.sum(jnp.where(eye, extra_col[keep, lane, :], 0.0), axis=0, keepdims=True)
            filt_ref[2 * keep : 2 * keep + 1, lane] = f
            smooth_ref[2 * keep : 2 * keep + 1, lane] = f + e
            at = pl.ds(4 * (2 * (first + keep) + 1) + b, 1)
            f = filt_row[at, :]
            filt_ref[2 * keep + 1 : 2 * keep + 2, lane] = f
            smooth_ref[2 * keep + 1 : 2 * keep + 2, lane] = f + extra_row[at, :]


def smoother(op, val, wgt, step, block, live, transition, predicted_precision, starting_mean, segments):
    tiles = op.shape[0]
    width = transition.shape[0]
    times = segments // 4
    hbm, vmem = pl.BlockSpec(memory_space=pltpu.HBM), pl.BlockSpec(memory_space=pltpu.VMEM)
    shape = jax.ShapeDtypeStruct((4, width), F32)
    return pl.pallas_call(
        tile_kernel,
        out_shape=(shape, shape),
        in_specs=[hbm] * 9,
        out_specs=(vmem, vmem),
        scratch_shapes=[
            pltpu.VMEM((2 * segments, TILE), F32),
            pltpu.VMEM((width, width), F32),
            pltpu.VMEM((width, width), F32),
            pltpu.VMEM((4, TILE), F32),
            pltpu.VMEM((4, TILE), F32),
            pltpu.VMEM((tiles, TILE, TILE), BF16),
            pltpu.VMEM((tiles, TILE), BF16),
            pltpu.VMEM((tiles, TILE), F32),
            pltpu.VMEM((1, tiles), jnp.int32),
            pltpu.VMEM((1, tiles), jnp.int32),
            pltpu.VMEM((1, tiles), jnp.int32),
            pltpu.VMEM((tiles // 8, 32, TILE), F32),
            pltpu.VMEM((tiles, TILE), F32),
            pltpu.VMEM((tiles, TILE), F32),
            pltpu.VMEM((2 * segments, TILE), F32),
            pltpu.SemaphoreType.DMA((8,)),
            pltpu.SemaphoreType.DMA((PARTS,)),
            pltpu.VMEM((segments, TILE), F32),
            pltpu.VMEM((segments, TILE), F32),
            pltpu.VMEM((segments, TILE), F32),
            pltpu.VMEM((segments // 32, TILE), F32),
            pltpu.VMEM((segments // 32, TILE), F32),
            pltpu.SemaphoreType.DMA((10,)),
            pltpu.VMEM((segments, TILE), F32),
            pltpu.VMEM((segments, TILE), F32),
            pltpu.VMEM((4, times // 2, TILE), F32),
            pltpu.VMEM((4, times // 2, TILE), F32),
            pltpu.VMEM((times // 2, width, TILE), F32),
            pltpu.VMEM((times // 2, width, TILE), F32),
            pltpu.VMEM((segments, TILE), F32),
            pltpu.VMEM((segments, TILE), F32),
            pltpu.VMEM((segments, TILE), F32),
            pltpu.VMEM((2, width, TILE), F32),
            pltpu.VMEM((2, width, TILE), F32),
        ],
        compiler_params=pltpu.CompilerParams(
            collective_id=0, has_side_effects=True, vmem_limit_bytes=62 << 20
        ),
    )(
        op,
        val,
        wgt,
        step.reshape(1, -1),
        block.reshape(1, -1),
        live.reshape(1, -1),
        transition,
        predicted_precision.reshape(4, TILE),
        starting_mean.reshape(4, TILE),
    )


def shards(op, val, wgt, step, block, live, transition, predicted_precision, starting_mean):
    segments = 4 * 4 * lax.axis_size("tm")
    return smoother(
        op, val, wgt, step, block, live, transition, predicted_precision, starting_mean, segments
    )


def solution(mesh):
    both = ("tm", "sensor")
    in_specs = (P(both, None, None), P(both, None), P(both, None), P(both), P(both), P(both), P(), P(), P())
    out_specs = (P("tm", None), P("tm", None))
    return jax.shard_map(shards, mesh=mesh, in_specs=in_specs, out_specs=out_specs, check_vma=False)
```

```python
import functools
import itertools

import jax
import jax.numpy as jnp
from jax import lax
from jax.experimental import pallas as pl
from jax.experimental.pallas import tpu as pltpu
from jax.sharding import PartitionSpec as P

MESH = pl.DeviceIdType.MESH
TILE = 128
GROUPS = (("c",), ("y", "x", "z"))
SIZES = {"c": 2, "x": 4, "y": 4, "z": 4}
CHUNK = 128
PARTS = 8
F32, BF16 = jnp.float32, jnp.bfloat16


def parts(value):
    upper = value.astype(BF16)
    return upper, (value - upper.astype(F32)).astype(BF16)


def coordinates():
    tm = lax.axis_index("tm")
    mine = {
        "c": lax.rem(tm, 2),
        "x": lax.rem(lax.div(tm, 2), 4),
        "y": lax.div(tm, 8),
        "z": lax.axis_index("sensor"),
    }
    return {
        axis: [mine[axis]] + [lax.rem(mine[axis] + k, size) for k in range(1, size)]
        for axis, size in SIZES.items()
    }


def hops(offsets):
    return sum(min(offset, 4 - offset) for offset in offsets)


def team(group):
    every = list(itertools.product(*[range(SIZES[axis]) for axis in group]))[1:]
    return sorted(every, key=hops, reverse=True)


def size_of(group):
    return len(team(group)) + 1


def member(near, group, offsets):
    at = {axis: near[axis][0] for axis in SIZES}
    for axis, offset in zip(group, offsets):
        at[axis] = near[axis][offset]
    return at


def device_of(at):
    return (at["y"] * 8 + at["x"] * 2 + at["c"], at["z"])


def index_in(group, at):
    index = 0
    for axis in group:
        index = index * SIZES[axis] + at[axis]
    return index


def greet_all(near):
    barrier = pltpu.get_barrier_semaphore()
    for group in GROUPS:
        for offsets in team(group):
            to = device_of(member(near, group, offsets))
            pl.semaphore_signal(barrier, inc=1, device_id=to, device_id_type=MESH)


def wait_all():
    pl.semaphore_wait(pltpu.get_barrier_semaphore(), sum(size_of(group) - 1 for group in GROUPS))


def scatter(near, source, stage, rows, box, send, recv):
    group = GROUPS[stage]
    for k, offsets in enumerate(team(group)):
        to = member(near, group, offsets)
        pltpu.make_async_remote_copy(
            src_ref=source.at[pl.ds(pl.multiple_of(index_in(group, to) * rows, 8), rows)],
            dst_ref=box.at[pl.ds(k * rows, rows)],
            send_sem=send.at[stage],
            recv_sem=recv.at[stage],
            device_id=device_of(to),
            device_id_type=MESH,
        ).start()


def spread(near, out_ref, start, stage, rows, send, recv):
    group = GROUPS[stage]
    piece = out_ref.at[pl.ds(pl.multiple_of(start, 8), rows)]
    for offsets in team(group):
        pltpu.make_async_remote_copy(
            src_ref=piece,
            dst_ref=piece,
            send_sem=send.at[stage],
            recv_sem=recv.at[stage],
            device_id=device_of(member(near, group, offsets)),
            device_id_type=MESH,
        ).start()


def wait_bytes(box, sem):
    pltpu.make_async_copy(box, box, sem).wait()


def exchange(near, source, out_ref, works, boxes, send_in, recv_in, send_out, recv_out, meanwhile):
    count = len(GROUPS)
    start, starts = 0, []
    for stage, group in enumerate(GROUPS):
        size = size_of(group)
        rows = source.shape[0] // size
        box = boxes[stage]
        scatter(near, source, stage, rows, box, send_in, recv_in)
        me = pl.multiple_of(index_in(group, {axis: near[axis][0] for axis in SIZES}) * rows, 8)
        if stage == count - 1:
            meanwhile()
        wait_bytes(box, recv_in.at[stage])
        own = source[pl.ds(me, rows), :]
        works[stage][...] = own + jnp.sum(box[...].reshape(size - 1, rows, TILE), axis=0)
        start = start + me
        starts.append(start)
        source = works[stage]

    out_ref[pl.ds(pl.multiple_of(start, 8), source.shape[0]), :] = source[...]
    for stage in reversed(range(count)):
        spread(near, out_ref, starts[stage], stage, works[stage].shape[0], send_out, recv_out)
        wait_bytes(boxes[stage], recv_out.at[stage])
    for stage in range(count):
        wait_bytes(boxes[stage], send_in.at[stage])
        wait_bytes(boxes[stage], send_out.at[stage])


def tile_kernel(
    op_ref, val_hbm, wgt_hbm, step_hbm, block_hbm, live_hbm, tran_hbm, prec_hbm, start_hbm,
    both_ref,
    out_ref, tran_ref, flip_ref, prec_ref, start_ref, tiles_ref, val_ref, wgt_ref, step_ref, block_ref, live_ref, lhs, info, curv, local, small_sem, tile_sem,
    *scratch,
):
    count = len(GROUPS)
    scratch, own = scratch[: 2 * count + 4], scratch[2 * count + 4 :]
    tiles = op_ref.shape[0]
    each = tiles // PARTS
    small = ((live_hbm, live_ref), (wgt_hbm, wgt_ref), (val_hbm, val_ref), (step_hbm, step_ref), (block_hbm, block_ref),
             (tran_hbm, tran_ref), (prec_hbm, prec_ref), (start_hbm, start_ref))
    small = [pltpu.make_async_copy(a, b, small_sem.at[k]) for k, (a, b) in enumerate(small)]
    for copy in small[:3]:
        copy.start()

    def load(k):
        at = pl.ds(pl.multiple_of(k * each, each), each)
        return pltpu.make_async_copy(op_ref.at[at], tiles_ref.at[at], tile_sem.at[k])

    for k in range(PARTS):
        load(k).start()
    for copy in small[3:]:
        copy.start()
    near = coordinates()
    greet_all(near)

    for copy in small[:3]:
        copy.wait()
    for half in range(tiles // TILE):
        rows = pl.ds(half * TILE, TILE)
        live_count = live_ref[:, half * TILE : (half + 1) * TILE].astype(F32)
        live_count = jnp.transpose(jnp.broadcast_to(live_count, (TILE, TILE)))
        columns = lax.broadcasted_iota(jnp.int32, (TILE, TILE), 1).astype(F32)
        live = jnp.where(columns < live_count, wgt_ref[rows, :], 0.0)
        weighted = (live * val_ref[rows, :].astype(F32)).astype(BF16).astype(F32)
        upper = live.astype(BF16).astype(F32)
        lower = live - upper
        for kind, value in enumerate((weighted, upper, lower, jnp.zeros_like(live))):
            lhs[pl.ds(half * TILE // 8, TILE // 8), kind * 8 : (kind + 1) * 8, :] = value.reshape(TILE // 8, 8, TILE)

    place = lax.broadcasted_iota(jnp.int32, (8, TILE), 0)

    def part_sums(k, carry):
        load(k).wait()
        for group in range(each // 8):
            left = lhs[k * (each // 8) + group].astype(BF16)
            info_sum = jnp.zeros((8, TILE), F32)
            curv_sum = jnp.zeros((8, TILE), F32)
            for j in range(8):
                op = tiles_ref[k * each + group * 8 + j]
                both = jnp.concatenate([op, op * op], axis=1)
                got = jnp.dot(left, both, preferred_element_type=F32)
                info_sum = jnp.where(place == j, got[0:8, :TILE], info_sum)
                curv_sum = jnp.where(place == j, got[8:16, TILE:] + got[16:24, TILE:], curv_sum)
            at = pl.ds(pl.multiple_of(k * each + group * 8, 8), 8)
            info[at, :] = info_sum
            curv[at, :] = curv_sum
        return carry

    lax.fori_loop(0, PARTS, part_sums, 0)

    for copy in small[3:5]:
        copy.wait()
    segments = out_ref.shape[0] // 2
    ids = step_ref[...] * 4 + block_ref[...]
    targets = lax.broadcasted_iota(jnp.int32, (segments, tiles), 0)
    onehot = jnp.where(targets == ids, 1.0, 0.0).astype(BF16)
    stack = jnp.concatenate(parts(info[...]) + parts(curv[...]), axis=1)
    sums = jnp.dot(onehot, stack, preferred_element_type=F32)
    inform = (sums[:, :TILE] + sums[:, TILE : 2 * TILE]).reshape(segments // 8, 1, 8, TILE)
    observed = (sums[:, 2 * TILE : 3 * TILE] + sums[:, 3 * TILE :]).reshape(segments // 8, 1, 8, TILE)
    local[...] = jnp.concatenate([inform, observed], axis=1).reshape(2 * segments, TILE)
    wait_all()

    def meanwhile():
        for copy in small[5:]:
            copy.wait()
        for i in range(tran_ref.shape[0] // TILE):
            for j in range(tran_ref.shape[0] // TILE):
                a, b = slice(i * TILE, (i + 1) * TILE), slice(j * TILE, (j + 1) * TILE)
                flip_ref[b, a] = jnp.transpose(tran_ref[a, b])

    exchange(near, local, out_ref, scratch[:count], scratch[count : 2 * count], *scratch[2 * count :], meanwhile)
    recurrence(out_ref, tran_ref, flip_ref, prec_ref, start_ref, both_ref, *own)


def recurrence(
    sums_ref, tran_ref, flip_ref, prec_ref, start_ref, both_ref,
    gain, drive, drive_on, drive_back, gain_col, diff_col, diff_row, filt_row, extra_row, filt_col, extra_col,
):
    segments = sums_ref.shape[0] // 2
    times = segments // 4
    half = times // 2
    width = tran_ref.shape[0]
    chunks = width // CHUNK
    first = lax.axis_index("tm") * 2

    pp = prec_ref[...]
    pp = jnp.concatenate([pp, pp], axis=0)[None]
    both = sums_ref[...].reshape(segments // 8, 2, 8, TILE)
    inform, observed = both[:, 0], both[:, 1]
    inverse = 1.0 / (pp + observed)
    gain[...] = (pp * inverse).reshape(segments, TILE)
    drive[...] = (inform * inverse).reshape(segments, TILE)
    even_gain = jnp.concatenate([gain[pl.ds(b, half, 8), :] for b in range(4)], axis=1)
    upper = even_gain.astype(BF16).astype(F32)
    stack = jnp.concatenate([upper, even_gain - upper], axis=0)
    turned = [jnp.transpose(stack[:, b * TILE : (b + 1) * TILE]) for b in range(4)]
    turned = jnp.concatenate(turned, axis=0).astype(BF16)
    lane = lax.rem(lax.broadcasted_iota(jnp.int32, (TILE, 2 * TILE), 0), half)
    pair = lax.div(lax.broadcasted_iota(jnp.int32, (TILE, 2 * TILE), 1), TILE)
    for n in range(half // 2):
        pick = jnp.where(lane == 2 * n + pair, 1.0, 0.0).astype(BF16)
        wide = jnp.dot(turned, pick, preferred_element_type=F32)
        gain_col[2 * n] = wide[:, :TILE]
        gain_col[2 * n + 1] = wide[:, TILE:]

    even_drive = jnp.concatenate([drive[pl.ds(b, half, 8), :] for b in range(4)], axis=1)
    upper, lower = parts(even_drive)
    both = jnp.concatenate([upper, lower], axis=0)
    for ref, moved in ((flip_ref, drive_on), (tran_ref, drive_back)):
        high, low = parts(ref[...])
        main = jnp.dot(both, high, preferred_element_type=F32)
        total = main[:half] + (main[half:] + jnp.dot(upper, low, preferred_element_type=F32))
        for b in range(4):
            moved[b] = total[:, b * TILE : (b + 1) * TILE]

    def part(ref, c, *lead):
        return ref[(*lead, slice(c * CHUNK, (c + 1) * CHUNK), slice(None))].reshape(CHUNK // 8, 8, TILE)

    def block(ref, c, b):
        return ref[c * CHUNK : (c + 1) * CHUNK, b * TILE : (b + 1) * TILE].reshape(CHUNK // 8, 8, TILE)

    def row_to_col(ref, wide, c):
        total = block(ref, c, 0) * wide[0]
        for b in range(1, 4):
            total += block(ref, c, b) * wide[b]
        return jnp.sum(total, axis=2, keepdims=True)

    def gather(ref, col, c, sums):
        for b in range(4):
            sums[b].append(jnp.sum(block(ref, c, b) * col, axis=0))

    def finish(pieces):
        while len(pieces) > 1:
            pieces = [sum(pieces[k : k + 2]) for k in range(0, len(pieces), 2)]
        return jnp.sum(pieces[0], axis=0, keepdims=True)

    def spread(row):
        return [jnp.broadcast_to(r, (8, TILE))[None] for r in row]

    def forward(keep, i, row):
        even, odd = 2 * i, 2 * i + 1
        wide = spread(row)
        sums = [[] for _ in range(4)]
        for c in range(chunks):
            rows = slice(c * CHUNK, (c + 1) * CHUNK)
            bare = row_to_col(tran_ref, wide, c)
            col = part(gain_col, c, i) * bare
            gather(flip_ref, col, c, sums)
            diff_col[i, rows, :] = (col - bare).reshape(CHUNK, TILE)
            if keep is not None:
                filt_col[keep, rows, :] = col.reshape(CHUNK, TILE)
        out = []
        for b in range(4):
            at = pl.ds(4 * odd + b, 1)
            moved = finish(sums[b]) + drive_on[b, pl.ds(i, 1), :]
            value = gain[at, :] * moved + drive[at, :]
            diff_row[at, :] = value - moved
            filt_row[at, :] = value
            out.append(value)
        return tuple(out)

    row = tuple(start_ref[b : b + 1, :] for b in range(4))
    plain = functools.partial(forward, None)
    row = lax.fori_loop(0, first, plain, row)
    row = forward(0, first, row)
    row = forward(1, first + 1, row)
    row = lax.fori_loop(first + 2, half, plain, row)

    def step_back(odd, sums, moved):
        back = []
        for b in range(4):
            at = pl.ds(4 * odd + b, 1)
            value = gain[at, :] * (finish(sums[b]) + moved[b])
            extra_row[at, :] = value
            back.append(value + diff_row[at, :])
        return tuple(back)

    wide = spread(row)
    sums = [[] for _ in range(4)]
    for c in range(chunks):
        gather(tran_ref, -row_to_col(tran_ref, wide, c), c, sums)
    gain[4 * (times - 1) :, :] = jnp.zeros((4, TILE), F32)
    row = step_back(times - 1, sums, [0.0] * 4)

    def backward(keep, i, row):
        wide = spread(row)
        sums = [[] for _ in range(4)]
        for c in range(chunks):
            col = part(gain_col, c, i) * row_to_col(flip_ref, wide, c)
            if keep is not None:
                extra_col[keep, c * CHUNK : (c + 1) * CHUNK, :] = col.reshape(CHUNK, TILE)
            if keep != 0:
                gather(tran_ref, col + part(diff_col, c, i), c, sums)
        if keep == 0:
            return row
        moved = [drive_back[b, pl.ds(i, 1), :] for b in range(4)]
        return step_back(2 * i - 1, sums, moved)

    row = lax.fori_loop(0, half - 2 - first, lambda n, r: backward(None, half - 1 - n, r), row)
    row = backward(1, first + 1, row)
    backward(0, first, row)

    eye = lax.broadcasted_iota(jnp.int32, (TILE, TILE), 0) == lax.broadcasted_iota(jnp.int32, (TILE, TILE), 1)
    for keep in range(2):
        for b in range(4):
            lane = slice(b * TILE, (b + 1) * TILE)
            f = jnp.sum(jnp.where(eye, filt_col[keep, lane, :], 0.0), axis=0, keepdims=True)
            f = f + drive[pl.ds(8 * (first + keep) + b, 1), :]
            e = jnp.sum(jnp.where(eye, extra_col[keep, lane, :], 0.0), axis=0, keepdims=True)
            both_ref[2 * keep : 2 * keep + 1, lane] = f
            both_ref[4 + 2 * keep : 5 + 2 * keep, lane] = e
            at = pl.ds(4 * (2 * (first + keep) + 1) + b, 1)
            f = filt_row[at, :]
            both_ref[2 * keep + 1 : 2 * keep + 2, lane] = f
            both_ref[5 + 2 * keep : 6 + 2 * keep, lane] = extra_row[at, :]


def smoother(op, val, wgt, step, block, live, transition, predicted_precision, starting_mean, segments):
    tiles = op.shape[0]
    width = transition.shape[0]
    times = segments // 4
    rows, works, boxes = 2 * segments, [], []
    for group in GROUPS:
        size = size_of(group)
        rows //= size
        works.append(pltpu.VMEM((rows, TILE), F32))
        boxes.append(pltpu.VMEM(((size - 1) * rows, TILE), F32))
    hbm, vmem = pl.BlockSpec(memory_space=pltpu.HBM), pl.BlockSpec(memory_space=pltpu.VMEM)
    both = pl.pallas_call(
        tile_kernel,
        out_shape=jax.ShapeDtypeStruct((8, width), F32),
        in_specs=[hbm] * 9,
        out_specs=vmem,
        scratch_shapes=[
            pltpu.VMEM((2 * segments, TILE), F32),
            pltpu.VMEM((width, width), F32),
            pltpu.VMEM((width, width), F32),
            pltpu.VMEM((4, TILE), F32),
            pltpu.VMEM((4, TILE), F32),
            pltpu.VMEM((tiles, TILE, TILE), BF16),
            pltpu.VMEM((tiles, TILE), BF16),
            pltpu.VMEM((tiles, TILE), F32),
            pltpu.VMEM((1, tiles), jnp.int32),
            pltpu.VMEM((1, tiles), jnp.int32),
            pltpu.VMEM((1, tiles), jnp.int32),
            pltpu.VMEM((tiles // 8, 32, TILE), F32),
            pltpu.VMEM((tiles, TILE), F32),
            pltpu.VMEM((tiles, TILE), F32),
            pltpu.VMEM((2 * segments, TILE), F32),
            pltpu.SemaphoreType.DMA((8,)),
            pltpu.SemaphoreType.DMA((PARTS,)),
            *works,
            *boxes,
            *[pltpu.SemaphoreType.DMA((len(GROUPS),))] * 4,
            pltpu.VMEM((segments, TILE), F32),
            pltpu.VMEM((segments, TILE), F32),
            pltpu.VMEM((4, times // 2, TILE), F32),
            pltpu.VMEM((4, times // 2, TILE), F32),
            pltpu.VMEM((times // 2, width, TILE), F32),
            pltpu.VMEM((times // 2, width, TILE), F32),
            pltpu.VMEM((segments, TILE), F32),
            pltpu.VMEM((segments, TILE), F32),
            pltpu.VMEM((segments, TILE), F32),
            pltpu.VMEM((2, width, TILE), F32),
            pltpu.VMEM((2, width, TILE), F32),
        ],
        compiler_params=pltpu.CompilerParams(
            collective_id=0, has_side_effects=True, vmem_limit_bytes=62 << 20
        ),
    )(
        op,
        val,
        wgt,
        step.reshape(1, -1),
        block.reshape(1, -1),
        live.reshape(1, -1),
        transition,
        predicted_precision.reshape(4, TILE),
        starting_mean.reshape(4, TILE),
    )
    return both[:4], both[:4] + both[4:]


def shards(op, val, wgt, step, block, live, transition, predicted_precision, starting_mean):
    segments = 4 * 4 * lax.axis_size("tm")
    return smoother(
        op, val, wgt, step, block, live, transition, predicted_precision, starting_mean, segments
    )


def solution(mesh):
    both = ("tm", "sensor")
    in_specs = (P(both, None, None), P(both, None), P(both, None), P(both), P(both), P(both), P(), P(), P())
    out_specs = (P("tm", None), P("tm", None))
    return jax.shard_map(shards, mesh=mesh, in_specs=in_specs, out_specs=out_specs, check_vma=False)
```

```python
import functools
import itertools

import jax
import jax.numpy as jnp
from jax import lax
from jax.experimental import pallas as pl
from jax.experimental.pallas import tpu as pltpu
from jax.sharding import PartitionSpec as P

MESH = pl.DeviceIdType.MESH
TILE = 128
GROUPS = (("c",), ("y", "x", "z"))
SIZES = {"c": 2, "x": 4, "y": 4, "z": 4}
CHUNK = 128
PARTS = 4
F32, BF16 = jnp.float32, jnp.bfloat16


def parts(value):
    upper = value.astype(BF16)
    return upper, (value - upper.astype(F32)).astype(BF16)


def coordinates():
    tm = lax.axis_index("tm")
    mine = {
        "c": lax.rem(tm, 2),
        "x": lax.rem(lax.div(tm, 2), 4),
        "y": lax.div(tm, 8),
        "z": lax.axis_index("sensor"),
    }
    return {
        axis: [mine[axis]] + [lax.rem(mine[axis] + k, size) for k in range(1, size)]
        for axis, size in SIZES.items()
    }


def hops(offsets):
    return sum(min(offset, 4 - offset) for offset in offsets)


def team(group):
    every = list(itertools.product(*[range(SIZES[axis]) for axis in group]))[1:]
    return sorted(every, key=hops, reverse=True)


def size_of(group):
    return len(team(group)) + 1


def member(near, group, offsets):
    at = {axis: near[axis][0] for axis in SIZES}
    for axis, offset in zip(group, offsets):
        at[axis] = near[axis][offset]
    return at


def device_of(at):
    return (at["y"] * 8 + at["x"] * 2 + at["c"], at["z"])


def index_in(group, at):
    index = 0
    for axis in group:
        index = index * SIZES[axis] + at[axis]
    return index


def greet_all(near):
    barrier = pltpu.get_barrier_semaphore()
    for group in GROUPS:
        for offsets in team(group):
            to = device_of(member(near, group, offsets))
            pl.semaphore_signal(barrier, inc=1, device_id=to, device_id_type=MESH)


def wait_all():
    pl.semaphore_wait(pltpu.get_barrier_semaphore(), sum(size_of(group) - 1 for group in GROUPS))


def scatter(near, source, stage, rows, box, send, recv):
    group = GROUPS[stage]
    for k, offsets in enumerate(team(group)):
        to = member(near, group, offsets)
        pltpu.make_async_remote_copy(
            src_ref=source.at[pl.ds(pl.multiple_of(index_in(group, to) * rows, 8), rows)],
            dst_ref=box.at[pl.ds(k * rows, rows)],
            send_sem=send.at[stage],
            recv_sem=recv.at[stage],
            device_id=device_of(to),
            device_id_type=MESH,
        ).start()


def spread(near, out_ref, start, stage, rows, send, recv):
    group = GROUPS[stage]
    piece = out_ref.at[pl.ds(pl.multiple_of(start, 8), rows)]
    for offsets in team(group):
        pltpu.make_async_remote_copy(
            src_ref=piece,
            dst_ref=piece,
            send_sem=send.at[stage],
            recv_sem=recv.at[stage],
            device_id=device_of(member(near, group, offsets)),
            device_id_type=MESH,
        ).start()


def wait_bytes(box, sem):
    pltpu.make_async_copy(box, box, sem).wait()


def exchange(near, source, out_ref, works, boxes, send_in, recv_in, send_out, recv_out, meanwhile):
    count = len(GROUPS)
    start, starts = 0, []
    for stage, group in enumerate(GROUPS):
        size = size_of(group)
        rows = source.shape[0] // size
        box = boxes[stage]
        scatter(near, source, stage, rows, box, send_in, recv_in)
        me = pl.multiple_of(index_in(group, {axis: near[axis][0] for axis in SIZES}) * rows, 8)
        if stage == count - 1:
            meanwhile()
        wait_bytes(box, recv_in.at[stage])
        own = source[pl.ds(me, rows), :]
        works[stage][...] = own + jnp.sum(box[...].reshape(size - 1, rows, TILE), axis=0)
        start = start + me
        starts.append(start)
        source = works[stage]

    out_ref[pl.ds(pl.multiple_of(start, 8), source.shape[0]), :] = source[...]
    for stage in reversed(range(count)):
        spread(near, out_ref, starts[stage], stage, works[stage].shape[0], send_out, recv_out)
        if stage > 0:
            wait_bytes(boxes[stage], recv_out.at[stage])

    def arrived():
        wait_bytes(boxes[0], recv_out.at[0])
        for stage in range(count):
            wait_bytes(boxes[stage], send_in.at[stage])
            wait_bytes(boxes[stage], send_out.at[stage])

    return arrived


def tile_kernel(
    op_ref, val_hbm, wgt_hbm, step_hbm, block_hbm, live_hbm, tran_hbm, prec_hbm, start_hbm,
    both_ref,
    out_ref, tran_ref, flip_ref, prec_ref, start_ref, tiles_ref, val_ref, wgt_ref, step_ref, block_ref, live_ref, lhs, info, curv, local, small_sem, tile_sem,
    *scratch,
):
    count = len(GROUPS)
    scratch, own = scratch[: 2 * count + 4], scratch[2 * count + 4 :]
    tiles = op_ref.shape[0]
    each = tiles // PARTS
    small = ((live_hbm, live_ref), (wgt_hbm, wgt_ref), (val_hbm, val_ref), (step_hbm, step_ref), (block_hbm, block_ref),
             (tran_hbm, tran_ref), (prec_hbm, prec_ref), (start_hbm, start_ref))
    small = [pltpu.make_async_copy(a, b, small_sem.at[k]) for k, (a, b) in enumerate(small)]
    for copy in small[:3]:
        copy.start()

    def load(k):
        at = pl.ds(pl.multiple_of(k * each, each), each)
        return pltpu.make_async_copy(op_ref.at[at], tiles_ref.at[at], tile_sem.at[k])

    for k in range(PARTS):
        load(k).start()
    for copy in small[3:]:
        copy.start()
    near = coordinates()
    greet_all(near)

    for copy in small[:3]:
        copy.wait()
    for half in range(tiles // TILE):
        rows = pl.ds(half * TILE, TILE)
        live_count = live_ref[:, half * TILE : (half + 1) * TILE].astype(F32)
        live_count = jnp.transpose(jnp.broadcast_to(live_count, (TILE, TILE)))
        columns = lax.broadcasted_iota(jnp.int32, (TILE, TILE), 1).astype(F32)
        live = jnp.where(columns < live_count, wgt_ref[rows, :], 0.0)
        weighted = (live * val_ref[rows, :].astype(F32)).astype(BF16).astype(F32)
        upper = live.astype(BF16).astype(F32)
        lower = live - upper
        for kind, value in enumerate((weighted, upper, lower, jnp.zeros_like(live))):
            lhs[pl.ds(half * TILE // 8, TILE // 8), kind * 8 : (kind + 1) * 8, :] = value.reshape(TILE // 8, 8, TILE)

    place = lax.broadcasted_iota(jnp.int32, (8, TILE), 0)

    def part_sums(k, carry):
        load(k).wait()
        for group in range(each // 8):
            left = lhs[k * (each // 8) + group].astype(BF16)
            info_sum = jnp.zeros((8, TILE), F32)
            curv_sum = jnp.zeros((8, TILE), F32)
            for j in range(8):
                op = tiles_ref[k * each + group * 8 + j]
                both = jnp.concatenate([op, op * op], axis=1)
                got = jnp.dot(left, both, preferred_element_type=F32)
                info_sum = jnp.where(place == j, got[0:8, :TILE], info_sum)
                curv_sum = jnp.where(place == j, got[8:16, TILE:] + got[16:24, TILE:], curv_sum)
            at = pl.ds(pl.multiple_of(k * each + group * 8, 8), 8)
            info[at, :] = info_sum
            curv[at, :] = curv_sum
        return carry

    lax.fori_loop(0, PARTS, part_sums, 0)

    for copy in small[3:5]:
        copy.wait()
    segments = out_ref.shape[0] // 2
    ids = step_ref[...] * 4 + block_ref[...]
    targets = lax.broadcasted_iota(jnp.int32, (segments, tiles), 0)
    onehot = jnp.where(targets == ids, 1.0, 0.0).astype(BF16)
    stack = jnp.concatenate(parts(info[...]) + parts(curv[...]), axis=1)
    sums = jnp.dot(onehot, stack, preferred_element_type=F32)
    inform = (sums[:, :TILE] + sums[:, TILE : 2 * TILE]).reshape(segments // 8, 1, 8, TILE)
    observed = (sums[:, 2 * TILE : 3 * TILE] + sums[:, 3 * TILE :]).reshape(segments // 8, 1, 8, TILE)
    local[...] = jnp.concatenate([inform, observed], axis=1).reshape(2 * segments, TILE)
    wait_all()

    def meanwhile():
        for copy in small[5:]:
            copy.wait()
        for i in range(tran_ref.shape[0] // TILE):
            for j in range(tran_ref.shape[0] // TILE):
                a, b = slice(i * TILE, (i + 1) * TILE), slice(j * TILE, (j + 1) * TILE)
                flip_ref[b, a] = jnp.transpose(tran_ref[a, b])

    arrived = exchange(near, local, out_ref, scratch[:count], scratch[count : 2 * count], *scratch[2 * count :], meanwhile)
    recurrence(arrived, own[0], out_ref, tran_ref, flip_ref, prec_ref, start_ref, both_ref, *own[1:])


def recurrence(
    arrived, part_gain, sums_ref, tran_ref, flip_ref, prec_ref, start_ref, both_ref,
    gain, drive, drive_on, drive_back, gain_col, diff_col, diff_row, filt_row, extra_row, filt_col, extra_col,
):
    segments = sums_ref.shape[0] // 2
    times = segments // 4
    half = times // 2
    width = tran_ref.shape[0]
    chunks = width // CHUNK
    first = lax.axis_index("tm") * 2

    pp = prec_ref[...]
    pp = jnp.concatenate([pp, pp], axis=0)[None]
    lane = lax.rem(lax.broadcasted_iota(jnp.int32, (half, 2 * TILE), 0), half // 2)
    pair = lax.div(lax.broadcasted_iota(jnp.int32, (half, 2 * TILE), 1), TILE)

    def prepare(part):
        rows = segments // 2
        both = sums_ref[pl.ds(pl.multiple_of(part * segments, 8), segments), :].reshape(rows // 8, 2, 8, TILE)
        inverse = 1.0 / (pp + both[:, 1])
        value = (pp * inverse).reshape(rows, TILE)
        here = pl.ds(pl.multiple_of(part * rows, 8), rows)
        gain[here, :] = value
        drive[here, :] = (both[:, 0] * inverse).reshape(rows, TILE)
        part_gain[...] = value
        even_gain = jnp.concatenate([part_gain[pl.ds(b, half // 2, 8), :] for b in range(4)], axis=1)
        upper = even_gain.astype(BF16).astype(F32)
        stack = jnp.concatenate([upper, even_gain - upper], axis=0)
        turned = [jnp.transpose(stack[:, b * TILE : (b + 1) * TILE]) for b in range(4)]
        turned = jnp.concatenate(turned, axis=0).astype(BF16)
        for n in range(half // 4):
            pick = jnp.where(lane == 2 * n + pair, 1.0, 0.0).astype(BF16)
            wide = jnp.dot(turned, pick, preferred_element_type=F32)
            gain_col[part * (half // 2) + 2 * n] = wide[:, :TILE]
            gain_col[part * (half // 2) + 2 * n + 1] = wide[:, TILE:]

    core = lax.rem(lax.axis_index("tm"), 2)
    prepare(core)
    arrived()
    prepare(1 - core)

    even_drive = jnp.concatenate([drive[pl.ds(b, half, 8), :] for b in range(4)], axis=1)
    upper, lower = parts(even_drive)
    both = jnp.concatenate([upper, lower], axis=0)
    for ref, moved in ((flip_ref, drive_on), (tran_ref, drive_back)):
        high, low = parts(ref[...])
        main = jnp.dot(both, high, preferred_element_type=F32)
        total = main[:half] + (main[half:] + jnp.dot(upper, low, preferred_element_type=F32))
        for b in range(4):
            moved[b] = total[:, b * TILE : (b + 1) * TILE]

    def part(ref, c, *lead):
        return ref[(*lead, slice(c * CHUNK, (c + 1) * CHUNK), slice(None))].reshape(CHUNK // 8, 8, TILE)

    def block(ref, c, b):
        return ref[c * CHUNK : (c + 1) * CHUNK, b * TILE : (b + 1) * TILE].reshape(CHUNK // 8, 8, TILE)

    def row_to_col(ref, wide, c):
        total = block(ref, c, 0) * wide[0]
        for b in range(1, 4):
            total += block(ref, c, b) * wide[b]
        return jnp.sum(total, axis=2, keepdims=True)

    def gather(ref, col, c, sums):
        for b in range(4):
            sums[b].append(jnp.sum(block(ref, c, b) * col, axis=0))

    def finish(pieces):
        while len(pieces) > 1:
            pieces = [sum(pieces[k : k + 2]) for k in range(0, len(pieces), 2)]
        return jnp.sum(pieces[0], axis=0, keepdims=True)

    def spread(row):
        return [jnp.broadcast_to(r, (8, TILE))[None] for r in row]

    def forward(keep, i, row):
        even, odd = 2 * i, 2 * i + 1
        wide = spread(row)
        sums = [[] for _ in range(4)]
        for c in range(chunks):
            rows = slice(c * CHUNK, (c + 1) * CHUNK)
            bare = row_to_col(tran_ref, wide, c)
            col = part(gain_col, c, i) * bare
            gather(flip_ref, col, c, sums)
            diff_col[i, rows, :] = (col - bare).reshape(CHUNK, TILE)
            if keep is not None:
                filt_col[keep, rows, :] = col.reshape(CHUNK, TILE)
        out = []
        for b in range(4):
            at = pl.ds(4 * odd + b, 1)
            moved = finish(sums[b]) + drive_on[b, pl.ds(i, 1), :]
            value = gain[at, :] * moved + drive[at, :]
            diff_row[at, :] = value - moved
            filt_row[at, :] = value
            out.append(value)
        return tuple(out)

    row = tuple(start_ref[b : b + 1, :] for b in range(4))
    plain = functools.partial(forward, None)
    row = lax.fori_loop(0, first, plain, row)
    row = forward(0, first, row)
    row = forward(1, first + 1, row)
    row = lax.fori_loop(first + 2, half, plain, row)

    def step_back(odd, sums, moved):
        back = []
        for b in range(4):
            at = pl.ds(4 * odd + b, 1)
            value = gain[at, :] * (finish(sums[b]) + moved[b])
            extra_row[at, :] = value
            back.append(value + diff_row[at, :])
        return tuple(back)

    wide = spread(row)
    sums = [[] for _ in range(4)]
    for c in range(chunks):
        gather(tran_ref, -row_to_col(tran_ref, wide, c), c, sums)
    gain[4 * (times - 1) :, :] = jnp.zeros((4, TILE), F32)
    row = step_back(times - 1, sums, [0.0] * 4)

    def backward(keep, i, row):
        wide = spread(row)
        sums = [[] for _ in range(4)]
        for c in range(chunks):
            col = part(gain_col, c, i) * row_to_col(flip_ref, wide, c)
            if keep is not None:
                extra_col[keep, c * CHUNK : (c + 1) * CHUNK, :] = col.reshape(CHUNK, TILE)
            if keep != 0:
                gather(tran_ref, col + part(diff_col, c, i), c, sums)
        if keep == 0:
            return row
        moved = [drive_back[b, pl.ds(i, 1), :] for b in range(4)]
        return step_back(2 * i - 1, sums, moved)

    row = lax.fori_loop(0, half - 2 - first, lambda n, r: backward(None, half - 1 - n, r), row)
    row = backward(1, first + 1, row)
    backward(0, first, row)

    eye = lax.broadcasted_iota(jnp.int32, (TILE, TILE), 0) == lax.broadcasted_iota(jnp.int32, (TILE, TILE), 1)
    for keep in range(2):
        for b in range(4):
            lane = slice(b * TILE, (b + 1) * TILE)
            f = jnp.sum(jnp.where(eye, filt_col[keep, lane, :], 0.0), axis=0, keepdims=True)
            f = f + drive[pl.ds(8 * (first + keep) + b, 1), :]
            e = jnp.sum(jnp.where(eye, extra_col[keep, lane, :], 0.0), axis=0, keepdims=True)
            both_ref[2 * keep : 2 * keep + 1, lane] = f
            both_ref[4 + 2 * keep : 5 + 2 * keep, lane] = e
            at = pl.ds(4 * (2 * (first + keep) + 1) + b, 1)
            f = filt_row[at, :]
            both_ref[2 * keep + 1 : 2 * keep + 2, lane] = f
            both_ref[5 + 2 * keep : 6 + 2 * keep, lane] = extra_row[at, :]


def smoother(op, val, wgt, step, block, live, transition, predicted_precision, starting_mean, segments):
    tiles = op.shape[0]
    width = transition.shape[0]
    times = segments // 4
    rows, works, boxes = 2 * segments, [], []
    for group in GROUPS:
        size = size_of(group)
        rows //= size
        works.append(pltpu.VMEM((rows, TILE), F32))
        boxes.append(pltpu.VMEM(((size - 1) * rows, TILE), F32))
    hbm, vmem = pl.BlockSpec(memory_space=pltpu.HBM), pl.BlockSpec(memory_space=pltpu.VMEM)
    both = pl.pallas_call(
        tile_kernel,
        out_shape=jax.ShapeDtypeStruct((8, width), F32),
        in_specs=[hbm] * 9,
        out_specs=vmem,
        scratch_shapes=[
            pltpu.VMEM((2 * segments, TILE), F32),
            pltpu.VMEM((width, width), F32),
            pltpu.VMEM((width, width), F32),
            pltpu.VMEM((4, TILE), F32),
            pltpu.VMEM((4, TILE), F32),
            pltpu.VMEM((tiles, TILE, TILE), BF16),
            pltpu.VMEM((tiles, TILE), BF16),
            pltpu.VMEM((tiles, TILE), F32),
            pltpu.VMEM((1, tiles), jnp.int32),
            pltpu.VMEM((1, tiles), jnp.int32),
            pltpu.VMEM((1, tiles), jnp.int32),
            pltpu.VMEM((tiles // 8, 32, TILE), F32),
            pltpu.VMEM((tiles, TILE), F32),
            pltpu.VMEM((tiles, TILE), F32),
            pltpu.VMEM((2 * segments, TILE), F32),
            pltpu.SemaphoreType.DMA((8,)),
            pltpu.SemaphoreType.DMA((PARTS,)),
            *works,
            *boxes,
            *[pltpu.SemaphoreType.DMA((len(GROUPS),))] * 4,
            pltpu.VMEM((segments // 2, TILE), F32),
            pltpu.VMEM((segments, TILE), F32),
            pltpu.VMEM((segments, TILE), F32),
            pltpu.VMEM((4, times // 2, TILE), F32),
            pltpu.VMEM((4, times // 2, TILE), F32),
            pltpu.VMEM((times // 2, width, TILE), F32),
            pltpu.VMEM((times // 2, width, TILE), F32),
            pltpu.VMEM((segments, TILE), F32),
            pltpu.VMEM((segments, TILE), F32),
            pltpu.VMEM((segments, TILE), F32),
            pltpu.VMEM((2, width, TILE), F32),
            pltpu.VMEM((2, width, TILE), F32),
        ],
        compiler_params=pltpu.CompilerParams(
            collective_id=0, has_side_effects=True, vmem_limit_bytes=62 << 20
        ),
    )(
        op,
        val,
        wgt,
        step.reshape(1, -1),
        block.reshape(1, -1),
        live.reshape(1, -1),
        transition,
        predicted_precision.reshape(4, TILE),
        starting_mean.reshape(4, TILE),
    )
    return both[:4], both[:4] + both[4:]


def shards(op, val, wgt, step, block, live, transition, predicted_precision, starting_mean):
    segments = 4 * 4 * lax.axis_size("tm")
    return smoother(
        op, val, wgt, step, block, live, transition, predicted_precision, starting_mean, segments
    )


def solution(mesh):
    both = ("tm", "sensor")
    in_specs = (P(both, None, None), P(both, None), P(both, None), P(both), P(both), P(both), P(), P(), P())
    out_specs = (P("tm", None), P("tm", None))
    return jax.shard_map(shards, mesh=mesh, in_specs=in_specs, out_specs=out_specs, check_vma=False)
```

```python
import functools
import itertools

import jax
import jax.numpy as jnp
from jax import lax
from jax.experimental import pallas as pl
from jax.experimental.pallas import tpu as pltpu
from jax.sharding import PartitionSpec as P

MESH = pl.DeviceIdType.MESH
TILE = 128
GROUPS = (("c",), ("y", "x", "z"))
SIZES = {"c": 2, "x": 4, "y": 4, "z": 4}
CHUNK = 128
PARTS = 4
F32, BF16 = jnp.float32, jnp.bfloat16


def parts(value):
    upper = value.astype(BF16)
    return upper, (value - upper.astype(F32)).astype(BF16)


def coordinates():
    tm = lax.axis_index("tm")
    mine = {
        "c": lax.rem(tm, 2),
        "x": lax.rem(lax.div(tm, 2), 4),
        "y": lax.div(tm, 8),
        "z": lax.axis_index("sensor"),
    }
    return {
        axis: [mine[axis]] + [lax.rem(mine[axis] + k, size) for k in range(1, size)]
        for axis, size in SIZES.items()
    }


def hops(offsets):
    return sum(min(offset, 4 - offset) for offset in offsets)


def team(group):
    every = list(itertools.product(*[range(SIZES[axis]) for axis in group]))[1:]
    return sorted(every, key=hops, reverse=True)


def size_of(group):
    return len(team(group)) + 1


def member(near, group, offsets):
    at = {axis: near[axis][0] for axis in SIZES}
    for axis, offset in zip(group, offsets):
        at[axis] = near[axis][offset]
    return at


def device_of(at):
    return (at["y"] * 8 + at["x"] * 2 + at["c"], at["z"])


def index_in(group, at):
    index = 0
    for axis in group:
        index = index * SIZES[axis] + at[axis]
    return index


def greet_all(near):
    barrier = pltpu.get_barrier_semaphore()
    for group in GROUPS:
        for offsets in team(group):
            to = device_of(member(near, group, offsets))
            pl.semaphore_signal(barrier, inc=1, device_id=to, device_id_type=MESH)


def wait_all():
    pl.semaphore_wait(pltpu.get_barrier_semaphore(), sum(size_of(group) - 1 for group in GROUPS))


def spread(near, out_ref, start, stage, rows, send, recv):
    group = GROUPS[stage]
    piece = out_ref.at[pl.ds(pl.multiple_of(start, 8), rows)]
    for offsets in team(group):
        pltpu.make_async_remote_copy(
            src_ref=piece,
            dst_ref=piece,
            send_sem=send.at[stage],
            recv_sem=recv.at[stage],
            device_id=device_of(member(near, group, offsets)),
            device_id_type=MESH,
        ).start()


def wait_bytes(box, sem):
    pltpu.make_async_copy(box, box, sem).wait()


def exchange(near, source, out_ref, works, boxes, pair_send, pair_recv, send_in, recv_in, send_out, recv_out, meanwhile):
    count = len(GROUPS)
    mine = {axis: near[axis][0] for axis in SIZES}
    half_rows, piece_rows = works[0].shape[0], works[1].shape[0]
    block = half_rows // SIZES["y"]
    order = (2, 1, 3, 0)
    halves = [near["c"][k] * half_rows for k in range(2)]
    sibling = device_of(member(near, ("c",), (1,)))

    def block_at(base, offset):
        return pl.ds(pl.multiple_of(base + near["y"][offset] * block, 8), block)

    for k, offset in enumerate(order):
        pltpu.make_async_remote_copy(
            src_ref=source.at[block_at(halves[1], offset)],
            dst_ref=boxes[0].at[block_at(0, offset)],
            send_sem=pair_send.at[k],
            recv_sem=pair_recv.at[k],
            device_id=sibling,
            device_id_type=MESH,
        ).start()
    everyone = team(GROUPS[1])
    for k, offset in enumerate(order):
        here = block_at(0, offset)
        wait_bytes(boxes[0].at[here], pair_recv.at[k])
        works[0][here, :] = source[block_at(halves[0], offset), :] + boxes[0][here, :]
        for slot, offsets in enumerate(everyone):
            if offsets[0] == offset:
                to = member(near, GROUPS[1], offsets)
                at = pl.multiple_of(index_in(GROUPS[1], to) * piece_rows, 8)
                pltpu.make_async_remote_copy(
                    src_ref=works[0].at[pl.ds(at, piece_rows)],
                    dst_ref=boxes[1].at[pl.ds(slot * piece_rows, piece_rows)],
                    send_sem=send_in.at[1],
                    recv_sem=recv_in.at[1],
                    device_id=device_of(to),
                    device_id_type=MESH,
                ).start()
    meanwhile()
    wait_bytes(boxes[1], recv_in.at[1])
    me = index_in(GROUPS[1], mine) * piece_rows
    own = works[0][pl.ds(pl.multiple_of(me, 8), piece_rows), :]
    works[1][...] = own + jnp.sum(boxes[1][...].reshape(len(everyone), piece_rows, TILE), axis=0)
    starts = [halves[0], halves[0] + me]
    start, source = starts[1], works[1]

    out_ref[pl.ds(pl.multiple_of(start, 8), source.shape[0]), :] = source[...]
    for stage in reversed(range(count)):
        spread(near, out_ref, starts[stage], stage, works[stage].shape[0], send_out, recv_out)
        if stage > 0:
            wait_bytes(boxes[stage], recv_out.at[stage])

    def arrived():
        wait_bytes(boxes[0], recv_out.at[0])
        for k in range(SIZES["y"]):
            wait_bytes(boxes[0].at[pl.ds(0, block)], pair_send.at[k])
        wait_bytes(boxes[1], send_in.at[1])
        for stage in range(count):
            wait_bytes(boxes[stage], send_out.at[stage])

    return arrived


def tile_kernel(
    op_ref, val_hbm, wgt_hbm, step_hbm, block_hbm, live_hbm, tran_hbm, prec_hbm, start_hbm,
    both_ref,
    out_ref, tran_ref, flip_ref, prec_ref, start_ref, tiles_ref, val_ref, wgt_ref, step_ref, block_ref, live_ref, lhs, info, curv, local, small_sem, tile_sem,
    *scratch,
):
    count = len(GROUPS)
    scratch, own = scratch[: 2 * count + 6], scratch[2 * count + 6 :]
    tiles = op_ref.shape[0]
    each = tiles // PARTS
    small = ((live_hbm, live_ref), (wgt_hbm, wgt_ref), (val_hbm, val_ref), (step_hbm, step_ref), (block_hbm, block_ref),
             (tran_hbm, tran_ref), (prec_hbm, prec_ref), (start_hbm, start_ref))
    small = [pltpu.make_async_copy(a, b, small_sem.at[k]) for k, (a, b) in enumerate(small)]
    for copy in small[:3]:
        copy.start()

    def load(k):
        at = pl.ds(pl.multiple_of(k * each, each), each)
        return pltpu.make_async_copy(op_ref.at[at], tiles_ref.at[at], tile_sem.at[k])

    for k in range(PARTS):
        load(k).start()
    for copy in small[3:]:
        copy.start()
    near = coordinates()
    greet_all(near)

    for copy in small[:3]:
        copy.wait()
    for half in range(tiles // TILE):
        rows = pl.ds(half * TILE, TILE)
        live_count = live_ref[:, half * TILE : (half + 1) * TILE].astype(F32)
        live_count = jnp.transpose(jnp.broadcast_to(live_count, (TILE, TILE)))
        columns = lax.broadcasted_iota(jnp.int32, (TILE, TILE), 1).astype(F32)
        live = jnp.where(columns < live_count, wgt_ref[rows, :], 0.0)
        weighted = (live * val_ref[rows, :].astype(F32)).astype(BF16).astype(F32)
        upper = live.astype(BF16).astype(F32)
        lower = live - upper
        for kind, value in enumerate((weighted, upper, lower, jnp.zeros_like(live))):
            lhs[pl.ds(half * TILE // 8, TILE // 8), kind * 8 : (kind + 1) * 8, :] = value.reshape(TILE // 8, 8, TILE)

    place = lax.broadcasted_iota(jnp.int32, (8, TILE), 0)

    def part_sums(k, carry):
        load(k).wait()
        for group in range(each // 8):
            left = lhs[k * (each // 8) + group].astype(BF16)
            info_sum = jnp.zeros((8, TILE), F32)
            curv_sum = jnp.zeros((8, TILE), F32)
            for j in range(8):
                op = tiles_ref[k * each + group * 8 + j]
                both = jnp.concatenate([op, op * op], axis=1)
                got = jnp.dot(left, both, preferred_element_type=F32)
                info_sum = jnp.where(place == j, got[0:8, :TILE], info_sum)
                curv_sum = jnp.where(place == j, got[8:16, TILE:] + got[16:24, TILE:], curv_sum)
            at = pl.ds(pl.multiple_of(k * each + group * 8, 8), 8)
            info[at, :] = info_sum
            curv[at, :] = curv_sum
        return carry

    lax.fori_loop(0, PARTS, part_sums, 0)

    for copy in small[3:5]:
        copy.wait()
    segments = out_ref.shape[0] // 2
    ids = step_ref[...] * 4 + block_ref[...]
    targets = lax.broadcasted_iota(jnp.int32, (segments, tiles), 0)
    onehot = jnp.where(targets == ids, 1.0, 0.0).astype(BF16)
    stack = jnp.concatenate(parts(info[...]) + parts(curv[...]), axis=1)
    sums = jnp.dot(onehot, stack, preferred_element_type=F32)
    inform = (sums[:, :TILE] + sums[:, TILE : 2 * TILE]).reshape(segments // 8, 1, 8, TILE)
    observed = (sums[:, 2 * TILE : 3 * TILE] + sums[:, 3 * TILE :]).reshape(segments // 8, 1, 8, TILE)
    local[...] = jnp.concatenate([inform, observed], axis=1).reshape(2 * segments, TILE)
    wait_all()

    def meanwhile():
        for copy in small[5:]:
            copy.wait()
        for i in range(tran_ref.shape[0] // TILE):
            for j in range(tran_ref.shape[0] // TILE):
                a, b = slice(i * TILE, (i + 1) * TILE), slice(j * TILE, (j + 1) * TILE)
                flip_ref[b, a] = jnp.transpose(tran_ref[a, b])

    arrived = exchange(near, local, out_ref, scratch[:count], scratch[count : 2 * count], *scratch[2 * count :], meanwhile)
    recurrence(arrived, own[0], out_ref, tran_ref, flip_ref, prec_ref, start_ref, both_ref, *own[1:])


def recurrence(
    arrived, part_gain, sums_ref, tran_ref, flip_ref, prec_ref, start_ref, both_ref,
    gain, drive, drive_on, drive_back, gain_col, diff_col, diff_row, filt_row, extra_row, filt_col, extra_col,
):
    segments = sums_ref.shape[0] // 2
    times = segments // 4
    half = times // 2
    width = tran_ref.shape[0]
    chunks = width // CHUNK
    first = lax.axis_index("tm") * 2

    pp = prec_ref[...]
    pp = jnp.concatenate([pp, pp], axis=0)[None]
    lane = lax.rem(lax.broadcasted_iota(jnp.int32, (half, 2 * TILE), 0), half // 2)
    pair = lax.div(lax.broadcasted_iota(jnp.int32, (half, 2 * TILE), 1), TILE)

    def prepare(part):
        rows = segments // 2
        both = sums_ref[pl.ds(pl.multiple_of(part * segments, 8), segments), :].reshape(rows // 8, 2, 8, TILE)
        inverse = 1.0 / (pp + both[:, 1])
        value = (pp * inverse).reshape(rows, TILE)
        here = pl.ds(pl.multiple_of(part * rows, 8), rows)
        gain[here, :] = value
        drive[here, :] = (both[:, 0] * inverse).reshape(rows, TILE)
        part_gain[...] = value
        even_gain = jnp.concatenate([part_gain[pl.ds(b, half // 2, 8), :] for b in range(4)], axis=1)
        upper = even_gain.astype(BF16).astype(F32)
        stack = jnp.concatenate([upper, even_gain - upper], axis=0)
        turned = [jnp.transpose(stack[:, b * TILE : (b + 1) * TILE]) for b in range(4)]
        turned = jnp.concatenate(turned, axis=0).astype(BF16)
        for n in range(half // 4):
            pick = jnp.where(lane == 2 * n + pair, 1.0, 0.0).astype(BF16)
            wide = jnp.dot(turned, pick, preferred_element_type=F32)
            gain_col[part * (half // 2) + 2 * n] = wide[:, :TILE]
            gain_col[part * (half // 2) + 2 * n + 1] = wide[:, TILE:]

    core = lax.rem(lax.axis_index("tm"), 2)
    prepare(core)
    arrived()
    prepare(1 - core)

    even_drive = jnp.concatenate([drive[pl.ds(b, half, 8), :] for b in range(4)], axis=1)
    upper, lower = parts(even_drive)
    both = jnp.concatenate([upper, lower], axis=0)
    for ref, moved in ((flip_ref, drive_on), (tran_ref, drive_back)):
        high, low = parts(ref[...])
        main = jnp.dot(both, high, preferred_element_type=F32)
        total = main[:half] + (main[half:] + jnp.dot(upper, low, preferred_element_type=F32))
        for b in range(4):
            moved[b] = total[:, b * TILE : (b + 1) * TILE]

    def part(ref, c, *lead):
        return ref[(*lead, slice(c * CHUNK, (c + 1) * CHUNK), slice(None))].reshape(CHUNK // 8, 8, TILE)

    def block(ref, c, b):
        return ref[c * CHUNK : (c + 1) * CHUNK, b * TILE : (b + 1) * TILE].reshape(CHUNK // 8, 8, TILE)

    def row_to_col(ref, wide, c):
        total = block(ref, c, 0) * wide[0]
        for b in range(1, 4):
            total += block(ref, c, b) * wide[b]
        return jnp.sum(total, axis=2, keepdims=True)

    def gather(ref, col, c, sums):
        for b in range(4):
            sums[b].append(jnp.sum(block(ref, c, b) * col, axis=0))

    def finish(pieces):
        while len(pieces) > 1:
            pieces = [sum(pieces[k : k + 2]) for k in range(0, len(pieces), 2)]
        return jnp.sum(pieces[0], axis=0, keepdims=True)

    def spread(row):
        return [jnp.broadcast_to(r, (8, TILE))[None] for r in row]

    def forward(keep, i, row):
        even, odd = 2 * i, 2 * i + 1
        wide = spread(row)
        sums = [[] for _ in range(4)]
        for c in range(chunks):
            rows = slice(c * CHUNK, (c + 1) * CHUNK)
            bare = row_to_col(tran_ref, wide, c)
            col = part(gain_col, c, i) * bare
            gather(flip_ref, col, c, sums)
            diff_col[i, rows, :] = (col - bare).reshape(CHUNK, TILE)
            if keep is not None:
                filt_col[keep, rows, :] = col.reshape(CHUNK, TILE)
        out = []
        for b in range(4):
            at = pl.ds(4 * odd + b, 1)
            moved = finish(sums[b]) + drive_on[b, pl.ds(i, 1), :]
            value = gain[at, :] * moved + drive[at, :]
            diff_row[at, :] = value - moved
            filt_row[at, :] = value
            out.append(value)
        return tuple(out)

    row = tuple(start_ref[b : b + 1, :] for b in range(4))
    plain = functools.partial(forward, None)
    row = lax.fori_loop(0, first, plain, row)
    row = forward(0, first, row)
    row = forward(1, first + 1, row)
    row = lax.fori_loop(first + 2, half, plain, row)

    def step_back(odd, sums, moved):
        back = []
        for b in range(4):
            at = pl.ds(4 * odd + b, 1)
            value = gain[at, :] * (finish(sums[b]) + moved[b])
            extra_row[at, :] = value
            back.append(value + diff_row[at, :])
        return tuple(back)

    wide = spread(row)
    sums = [[] for _ in range(4)]
    for c in range(chunks):
        gather(tran_ref, -row_to_col(tran_ref, wide, c), c, sums)
    gain[4 * (times - 1) :, :] = jnp.zeros((4, TILE), F32)
    row = step_back(times - 1, sums, [0.0] * 4)

    def backward(keep, i, row):
        wide = spread(row)
        sums = [[] for _ in range(4)]
        for c in range(chunks):
            col = part(gain_col, c, i) * row_to_col(flip_ref, wide, c)
            if keep is not None:
                extra_col[keep, c * CHUNK : (c + 1) * CHUNK, :] = col.reshape(CHUNK, TILE)
            if keep != 0:
                gather(tran_ref, col + part(diff_col, c, i), c, sums)
        if keep == 0:
            return row
        moved = [drive_back[b, pl.ds(i, 1), :] for b in range(4)]
        return step_back(2 * i - 1, sums, moved)

    row = lax.fori_loop(0, half - 2 - first, lambda n, r: backward(None, half - 1 - n, r), row)
    row = backward(1, first + 1, row)
    backward(0, first, row)

    eye = lax.broadcasted_iota(jnp.int32, (TILE, TILE), 0) == lax.broadcasted_iota(jnp.int32, (TILE, TILE), 1)
    for keep in range(2):
        for b in range(4):
            lane = slice(b * TILE, (b + 1) * TILE)
            f = jnp.sum(jnp.where(eye, filt_col[keep, lane, :], 0.0), axis=0, keepdims=True)
            f = f + drive[pl.ds(8 * (first + keep) + b, 1), :]
            e = jnp.sum(jnp.where(eye, extra_col[keep, lane, :], 0.0), axis=0, keepdims=True)
            both_ref[2 * keep : 2 * keep + 1, lane] = f
            both_ref[4 + 2 * keep : 5 + 2 * keep, lane] = e
            at = pl.ds(4 * (2 * (first + keep) + 1) + b, 1)
            f = filt_row[at, :]
            both_ref[2 * keep + 1 : 2 * keep + 2, lane] = f
            both_ref[5 + 2 * keep : 6 + 2 * keep, lane] = extra_row[at, :]


def smoother(op, val, wgt, step, block, live, transition, predicted_precision, starting_mean, segments):
    tiles = op.shape[0]
    width = transition.shape[0]
    times = segments // 4
    rows, works, boxes = 2 * segments, [], []
    for group in GROUPS:
        size = size_of(group)
        rows //= size
        works.append(pltpu.VMEM((rows, TILE), F32))
        boxes.append(pltpu.VMEM(((size - 1) * rows, TILE), F32))
    hbm, vmem = pl.BlockSpec(memory_space=pltpu.HBM), pl.BlockSpec(memory_space=pltpu.VMEM)
    both = pl.pallas_call(
        tile_kernel,
        out_shape=jax.ShapeDtypeStruct((8, width), F32),
        in_specs=[hbm] * 9,
        out_specs=vmem,
        scratch_shapes=[
            pltpu.VMEM((2 * segments, TILE), F32),
            pltpu.VMEM((width, width), F32),
            pltpu.VMEM((width, width), F32),
            pltpu.VMEM((4, TILE), F32),
            pltpu.VMEM((4, TILE), F32),
            pltpu.VMEM((tiles, TILE, TILE), BF16),
            pltpu.VMEM((tiles, TILE), BF16),
            pltpu.VMEM((tiles, TILE), F32),
            pltpu.VMEM((1, tiles), jnp.int32),
            pltpu.VMEM((1, tiles), jnp.int32),
            pltpu.VMEM((1, tiles), jnp.int32),
            pltpu.VMEM((tiles // 8, 32, TILE), F32),
            pltpu.VMEM((tiles, TILE), F32),
            pltpu.VMEM((tiles, TILE), F32),
            pltpu.VMEM((2 * segments, TILE), F32),
            pltpu.SemaphoreType.DMA((8,)),
            pltpu.SemaphoreType.DMA((PARTS,)),
            *works,
            *boxes,
            *[pltpu.SemaphoreType.DMA((SIZES["y"],))] * 2,
            *[pltpu.SemaphoreType.DMA((len(GROUPS),))] * 4,
            pltpu.VMEM((segments // 2, TILE), F32),
            pltpu.VMEM((segments, TILE), F32),
            pltpu.VMEM((segments, TILE), F32),
            pltpu.VMEM((4, times // 2, TILE), F32),
            pltpu.VMEM((4, times // 2, TILE), F32),
            pltpu.VMEM((times // 2, width, TILE), F32),
            pltpu.VMEM((times // 2, width, TILE), F32),
            pltpu.VMEM((segments, TILE), F32),
            pltpu.VMEM((segments, TILE), F32),
            pltpu.VMEM((segments, TILE), F32),
            pltpu.VMEM((2, width, TILE), F32),
            pltpu.VMEM((2, width, TILE), F32),
        ],
        compiler_params=pltpu.CompilerParams(
            collective_id=0, has_side_effects=True, vmem_limit_bytes=62 << 20
        ),
    )(
        op,
        val,
        wgt,
        step.reshape(1, -1),
        block.reshape(1, -1),
        live.reshape(1, -1),
        transition,
        predicted_precision.reshape(4, TILE),
        starting_mean.reshape(4, TILE),
    )
    return both[:4], both[:4] + both[4:]


def shards(op, val, wgt, step, block, live, transition, predicted_precision, starting_mean):
    segments = 4 * 4 * lax.axis_size("tm")
    return smoother(
        op, val, wgt, step, block, live, transition, predicted_precision, starting_mean, segments
    )


def solution(mesh):
    both = ("tm", "sensor")
    in_specs = (P(both, None, None), P(both, None), P(both, None), P(both), P(both), P(both), P(), P(), P())
    out_specs = (P("tm", None), P("tm", None))
    return jax.shard_map(shards, mesh=mesh, in_specs=in_specs, out_specs=out_specs, check_vma=False)
```

```python
import functools
import itertools

import jax
import jax.numpy as jnp
from jax import lax
from jax.experimental import pallas as pl
from jax.experimental.pallas import tpu as pltpu
from jax.sharding import PartitionSpec as P

MESH = pl.DeviceIdType.MESH
TILE = 128
GROUPS = (("c",), ("y", "x", "z"))
SIZES = {"c": 2, "x": 4, "y": 4, "z": 4}
CHUNK = 32
DEPTH = 2
ACCS = 1
PARTS = 4
F32, BF16 = jnp.float32, jnp.bfloat16


def parts(value):
    upper = value.astype(BF16)
    return upper, (value - upper.astype(F32)).astype(BF16)


def coordinates():
    tm = lax.axis_index("tm")
    mine = {
        "c": lax.rem(tm, 2),
        "x": lax.rem(lax.div(tm, 2), 4),
        "y": lax.div(tm, 8),
        "z": lax.axis_index("sensor"),
    }
    return {
        axis: [mine[axis]] + [lax.rem(mine[axis] + k, size) for k in range(1, size)]
        for axis, size in SIZES.items()
    }


def hops(offsets):
    return sum(min(offset, 4 - offset) for offset in offsets)


def team(group):
    every = list(itertools.product(*[range(SIZES[axis]) for axis in group]))[1:]
    return sorted(every, key=hops, reverse=True)


def size_of(group):
    return len(team(group)) + 1


def member(near, group, offsets):
    at = {axis: near[axis][0] for axis in SIZES}
    for axis, offset in zip(group, offsets):
        at[axis] = near[axis][offset]
    return at


def device_of(at):
    return (at["y"] * 8 + at["x"] * 2 + at["c"], at["z"])


def index_in(group, at):
    index = 0
    for axis in group:
        index = index * SIZES[axis] + at[axis]
    return index


def greet_all(near):
    barrier = pltpu.get_barrier_semaphore()
    for group in GROUPS:
        for offsets in team(group):
            to = device_of(member(near, group, offsets))
            pl.semaphore_signal(barrier, inc=1, device_id=to, device_id_type=MESH)


def wait_all():
    pl.semaphore_wait(pltpu.get_barrier_semaphore(), sum(size_of(group) - 1 for group in GROUPS))


def spread(near, out_ref, start, stage, rows, send, recv):
    group = GROUPS[stage]
    piece = out_ref.at[pl.ds(pl.multiple_of(start, 8), rows)]
    for offsets in team(group):
        pltpu.make_async_remote_copy(
            src_ref=piece,
            dst_ref=piece,
            send_sem=send.at[stage],
            recv_sem=recv.at[stage],
            device_id=device_of(member(near, group, offsets)),
            device_id_type=MESH,
        ).start()


def wait_bytes(box, sem):
    pltpu.make_async_copy(box, box, sem).wait()


def exchange(near, source, out_ref, works, boxes, pair_send, pair_recv, send_in, recv_in, send_out, recv_out, meanwhile):
    count = len(GROUPS)
    mine = {axis: near[axis][0] for axis in SIZES}
    half_rows, piece_rows = works[0].shape[0], works[1].shape[0]
    block = half_rows // SIZES["y"]
    order = (2, 1, 3, 0)
    halves = [near["c"][k] * half_rows for k in range(2)]
    sibling = device_of(member(near, ("c",), (1,)))

    def block_at(base, offset):
        return pl.ds(pl.multiple_of(base + near["y"][offset] * block, 8), block)

    for k, offset in enumerate(order):
        pltpu.make_async_remote_copy(
            src_ref=source.at[block_at(halves[1], offset)],
            dst_ref=boxes[0].at[block_at(0, offset)],
            send_sem=pair_send.at[k],
            recv_sem=pair_recv.at[k],
            device_id=sibling,
            device_id_type=MESH,
        ).start()
    everyone = team(GROUPS[1])
    for k, offset in enumerate(order):
        here = block_at(0, offset)
        wait_bytes(boxes[0].at[here], pair_recv.at[k])
        works[0][here, :] = source[block_at(halves[0], offset), :] + boxes[0][here, :]
        for slot, offsets in enumerate(everyone):
            if offsets[0] == offset:
                to = member(near, GROUPS[1], offsets)
                at = pl.multiple_of(index_in(GROUPS[1], to) * piece_rows, 8)
                pltpu.make_async_remote_copy(
                    src_ref=works[0].at[pl.ds(at, piece_rows)],
                    dst_ref=boxes[1].at[pl.ds(slot * piece_rows, piece_rows)],
                    send_sem=send_in.at[1],
                    recv_sem=recv_in.at[1],
                    device_id=device_of(to),
                    device_id_type=MESH,
                ).start()
    meanwhile()
    wait_bytes(boxes[1], recv_in.at[1])
    me = index_in(GROUPS[1], mine) * piece_rows
    own = works[0][pl.ds(pl.multiple_of(me, 8), piece_rows), :]
    works[1][...] = own + jnp.sum(boxes[1][...].reshape(len(everyone), piece_rows, TILE), axis=0)
    starts = [halves[0], halves[0] + me]
    start, source = starts[1], works[1]

    out_ref[pl.ds(pl.multiple_of(start, 8), source.shape[0]), :] = source[...]
    for stage in reversed(range(count)):
        spread(near, out_ref, starts[stage], stage, works[stage].shape[0], send_out, recv_out)
        if stage > 0:
            wait_bytes(boxes[stage], recv_out.at[stage])

    def arrived():
        wait_bytes(boxes[0], recv_out.at[0])
        for k in range(SIZES["y"]):
            wait_bytes(boxes[0].at[pl.ds(0, block)], pair_send.at[k])
        wait_bytes(boxes[1], send_in.at[1])
        for stage in range(count):
            wait_bytes(boxes[stage], send_out.at[stage])

    return arrived


def tile_kernel(
    op_ref, val_hbm, wgt_hbm, step_hbm, block_hbm, live_hbm, tran_hbm, prec_hbm, start_hbm,
    both_ref,
    out_ref, tran_ref, flip_ref, prec_ref, start_ref, tiles_ref, val_ref, wgt_ref, step_ref, block_ref, live_ref, lhs, info, curv, local, small_sem, tile_sem,
    *scratch,
):
    count = len(GROUPS)
    scratch, own = scratch[: 2 * count + 6], scratch[2 * count + 6 :]
    tiles = op_ref.shape[0]
    each = tiles // PARTS
    small = ((live_hbm, live_ref), (wgt_hbm, wgt_ref), (val_hbm, val_ref), (step_hbm, step_ref), (block_hbm, block_ref),
             (tran_hbm, tran_ref), (prec_hbm, prec_ref), (start_hbm, start_ref))
    small = [pltpu.make_async_copy(a, b, small_sem.at[k]) for k, (a, b) in enumerate(small)]
    for copy in small[:3]:
        copy.start()

    def load(k):
        at = pl.ds(pl.multiple_of(k * each, each), each)
        return pltpu.make_async_copy(op_ref.at[at], tiles_ref.at[at], tile_sem.at[k])

    for k in range(PARTS):
        load(k).start()
    for copy in small[3:]:
        copy.start()
    near = coordinates()
    greet_all(near)

    for copy in small[:3]:
        copy.wait()
    for half in range(tiles // TILE):
        rows = pl.ds(half * TILE, TILE)
        live_count = live_ref[:, half * TILE : (half + 1) * TILE].astype(F32)
        live_count = jnp.transpose(jnp.broadcast_to(live_count, (TILE, TILE)))
        columns = lax.broadcasted_iota(jnp.int32, (TILE, TILE), 1).astype(F32)
        live = jnp.where(columns < live_count, wgt_ref[rows, :], 0.0)
        weighted = (live * val_ref[rows, :].astype(F32)).astype(BF16).astype(F32)
        upper = live.astype(BF16).astype(F32)
        lower = live - upper
        for kind, value in enumerate((weighted, upper, lower, jnp.zeros_like(live))):
            lhs[pl.ds(half * TILE // 8, TILE // 8), kind * 8 : (kind + 1) * 8, :] = value.reshape(TILE // 8, 8, TILE)

    place = lax.broadcasted_iota(jnp.int32, (8, TILE), 0)

    def part_sums(k, carry):
        load(k).wait()
        for group in range(each // 8):
            left = lhs[k * (each // 8) + group].astype(BF16)
            info_sum = jnp.zeros((8, TILE), F32)
            curv_sum = jnp.zeros((8, TILE), F32)
            for j in range(8):
                op = tiles_ref[k * each + group * 8 + j]
                both = jnp.concatenate([op, op * op], axis=1)
                got = jnp.dot(left, both, preferred_element_type=F32)
                info_sum = jnp.where(place == j, got[0:8, :TILE], info_sum)
                curv_sum = jnp.where(place == j, got[8:16, TILE:] + got[16:24, TILE:], curv_sum)
            at = pl.ds(pl.multiple_of(k * each + group * 8, 8), 8)
            info[at, :] = info_sum
            curv[at, :] = curv_sum
        return carry

    lax.fori_loop(0, PARTS, part_sums, 0)

    for copy in small[3:5]:
        copy.wait()
    segments = out_ref.shape[0] // 2
    ids = step_ref[...] * 4 + block_ref[...]
    targets = lax.broadcasted_iota(jnp.int32, (segments, tiles), 0)
    onehot = jnp.where(targets == ids, 1.0, 0.0).astype(BF16)
    stack = jnp.concatenate(parts(info[...]) + parts(curv[...]), axis=1)
    sums = jnp.dot(onehot, stack, preferred_element_type=F32)
    inform = (sums[:, :TILE] + sums[:, TILE : 2 * TILE]).reshape(segments // 8, 1, 8, TILE)
    observed = (sums[:, 2 * TILE : 3 * TILE] + sums[:, 3 * TILE :]).reshape(segments // 8, 1, 8, TILE)
    local[...] = jnp.concatenate([inform, observed], axis=1).reshape(2 * segments, TILE)
    wait_all()

    def meanwhile():
        for copy in small[5:]:
            copy.wait()
        for i in range(tran_ref.shape[0] // TILE):
            for j in range(tran_ref.shape[0] // TILE):
                a, b = slice(i * TILE, (i + 1) * TILE), slice(j * TILE, (j + 1) * TILE)
                flip_ref[b, a] = jnp.transpose(tran_ref[a, b])

    arrived = exchange(near, local, out_ref, scratch[:count], scratch[count : 2 * count], *scratch[2 * count :], meanwhile)
    recurrence(arrived, own[0], out_ref, tran_ref, flip_ref, prec_ref, start_ref, both_ref, *own[1:])


def recurrence(
    arrived, part_gain, sums_ref, tran_ref, flip_ref, prec_ref, start_ref, both_ref,
    gain, drive, drive_on, drive_back, gain_col, diff_col, diff_row, filt_row, extra_row, filt_col, extra_col,
):
    segments = sums_ref.shape[0] // 2
    times = segments // 4
    half = times // 2
    width = tran_ref.shape[0]
    chunks = width // CHUNK
    first = lax.axis_index("tm") * 2

    pp = prec_ref[...]
    pp = jnp.concatenate([pp, pp], axis=0)[None]
    lane = lax.rem(lax.broadcasted_iota(jnp.int32, (half, 2 * TILE), 0), half // 2)
    pair = lax.div(lax.broadcasted_iota(jnp.int32, (half, 2 * TILE), 1), TILE)

    def prepare(part):
        rows = segments // 2
        both = sums_ref[pl.ds(pl.multiple_of(part * segments, 8), segments), :].reshape(rows // 8, 2, 8, TILE)
        inverse = 1.0 / (pp + both[:, 1])
        value = (pp * inverse).reshape(rows, TILE)
        here = pl.ds(pl.multiple_of(part * rows, 8), rows)
        gain[here, :] = value
        drive[here, :] = (both[:, 0] * inverse).reshape(rows, TILE)
        part_gain[...] = value
        even_gain = jnp.concatenate([part_gain[pl.ds(b, half // 2, 8), :] for b in range(4)], axis=1)
        upper = even_gain.astype(BF16).astype(F32)
        stack = jnp.concatenate([upper, even_gain - upper], axis=0)
        turned = [jnp.transpose(stack[:, b * TILE : (b + 1) * TILE]) for b in range(4)]
        turned = jnp.concatenate(turned, axis=0).astype(BF16)
        for n in range(half // 4):
            pick = jnp.where(lane == 2 * n + pair, 1.0, 0.0).astype(BF16)
            wide = jnp.dot(turned, pick, preferred_element_type=F32)
            gain_col[part * (half // 2) + 2 * n] = wide[:, :TILE]
            gain_col[part * (half // 2) + 2 * n + 1] = wide[:, TILE:]

    core = lax.rem(lax.axis_index("tm"), 2)
    prepare(core)
    arrived()
    prepare(1 - core)

    even_drive = jnp.concatenate([drive[pl.ds(b, half, 8), :] for b in range(4)], axis=1)
    upper, lower = parts(even_drive)
    both = jnp.concatenate([upper, lower], axis=0)
    for ref, moved in ((flip_ref, drive_on), (tran_ref, drive_back)):
        high, low = parts(ref[...])
        main = jnp.dot(both, high, preferred_element_type=F32)
        total = main[:half] + (main[half:] + jnp.dot(upper, low, preferred_element_type=F32))
        for b in range(4):
            moved[b] = total[:, b * TILE : (b + 1) * TILE]

    def part(ref, c, *lead):
        return ref[(*lead, slice(c * CHUNK, (c + 1) * CHUNK), slice(None))].reshape(CHUNK // 8, 8, TILE)

    def block(ref, c, b):
        return ref[c * CHUNK : (c + 1) * CHUNK, b * TILE : (b + 1) * TILE].reshape(CHUNK // 8, 8, TILE)

    def row_to_col(ref, wide, c):
        total = block(ref, c, 0) * wide[0]
        for b in range(1, 4):
            total += block(ref, c, b) * wide[b]
        return jnp.sum(total, axis=2, keepdims=True)

    def gather(ref, col, c, sums):
        for k in range(CHUNK // 8):
            for b in range(4):
                term = ref[c * CHUNK + 8 * k : c * CHUNK + 8 * k + 8, b * TILE : (b + 1) * TILE] * col[k]
                slot = k % ACCS
                if c == 0 and k < ACCS:
                    sums[b].append(term)
                else:
                    sums[b][slot] = sums[b][slot] + term

    def finish(pieces):
        while len(pieces) > 1:
            pieces = [sum(pieces[k : k + 2]) for k in range(0, len(pieces), 2)]
        return jnp.sum(pieces[0], axis=0, keepdims=True)

    def spread(row):
        return [jnp.broadcast_to(r, (8, TILE))[None] for r in row]

    def forward(keep, i, row):
        even, odd = 2 * i, 2 * i + 1
        wide = spread(row)
        sums = [[] for _ in range(4)]
        def use(c, bare):
            rows = slice(c * CHUNK, (c + 1) * CHUNK)
            col = part(gain_col, c, i) * bare
            gather(flip_ref, col, c, sums)
            diff_col[i, rows, :] = (col - bare).reshape(CHUNK, TILE)
            if keep is not None:
                filt_col[keep, rows, :] = col.reshape(CHUNK, TILE)

        pending = []
        for c in range(chunks):
            pending.append((c, row_to_col(tran_ref, wide, c)))
            if len(pending) > DEPTH:
                use(*pending.pop(0))
        for item in pending:
            use(*item)
        out = []
        for b in range(4):
            at = pl.ds(4 * odd + b, 1)
            moved = finish(sums[b]) + drive_on[b, pl.ds(i, 1), :]
            value = gain[at, :] * moved + drive[at, :]
            diff_row[at, :] = value - moved
            filt_row[at, :] = value
            out.append(value)
        return tuple(out)

    row = tuple(start_ref[b : b + 1, :] for b in range(4))
    plain = functools.partial(forward, None)
    row = lax.fori_loop(0, first, plain, row)
    row = forward(0, first, row)
    row = forward(1, first + 1, row)
    row = lax.fori_loop(first + 2, half, plain, row)

    def step_back(odd, sums, moved):
        back = []
        for b in range(4):
            at = pl.ds(4 * odd + b, 1)
            value = gain[at, :] * (finish(sums[b]) + moved[b])
            extra_row[at, :] = value
            back.append(value + diff_row[at, :])
        return tuple(back)

    wide = spread(row)
    sums = [[] for _ in range(4)]
    for c in range(chunks):
        gather(tran_ref, -row_to_col(tran_ref, wide, c), c, sums)
    gain[4 * (times - 1) :, :] = jnp.zeros((4, TILE), F32)
    row = step_back(times - 1, sums, [0.0] * 4)

    def backward(keep, i, row):
        wide = spread(row)
        sums = [[] for _ in range(4)]
        def use(c, bare):
            col = part(gain_col, c, i) * bare
            if keep is not None:
                extra_col[keep, c * CHUNK : (c + 1) * CHUNK, :] = col.reshape(CHUNK, TILE)
            if keep != 0:
                gather(tran_ref, col + part(diff_col, c, i), c, sums)

        pending = []
        for c in range(chunks):
            pending.append((c, row_to_col(flip_ref, wide, c)))
            if len(pending) > DEPTH:
                use(*pending.pop(0))
        for item in pending:
            use(*item)
        if keep == 0:
            return row
        moved = [drive_back[b, pl.ds(i, 1), :] for b in range(4)]
        return step_back(2 * i - 1, sums, moved)

    row = lax.fori_loop(0, half - 2 - first, lambda n, r: backward(None, half - 1 - n, r), row)
    row = backward(1, first + 1, row)
    backward(0, first, row)

    eye = lax.broadcasted_iota(jnp.int32, (TILE, TILE), 0) == lax.broadcasted_iota(jnp.int32, (TILE, TILE), 1)
    for keep in range(2):
        for b in range(4):
            lane = slice(b * TILE, (b + 1) * TILE)
            f = jnp.sum(jnp.where(eye, filt_col[keep, lane, :], 0.0), axis=0, keepdims=True)
            f = f + drive[pl.ds(8 * (first + keep) + b, 1), :]
            e = jnp.sum(jnp.where(eye, extra_col[keep, lane, :], 0.0), axis=0, keepdims=True)
            both_ref[2 * keep : 2 * keep + 1, lane] = f
            both_ref[4 + 2 * keep : 5 + 2 * keep, lane] = e
            at = pl.ds(4 * (2 * (first + keep) + 1) + b, 1)
            f = filt_row[at, :]
            both_ref[2 * keep + 1 : 2 * keep + 2, lane] = f
            both_ref[5 + 2 * keep : 6 + 2 * keep, lane] = extra_row[at, :]


def smoother(op, val, wgt, step, block, live, transition, predicted_precision, starting_mean, segments):
    tiles = op.shape[0]
    width = transition.shape[0]
    times = segments // 4
    rows, works, boxes = 2 * segments, [], []
    for group in GROUPS:
        size = size_of(group)
        rows //= size
        works.append(pltpu.VMEM((rows, TILE), F32))
        boxes.append(pltpu.VMEM(((size - 1) * rows, TILE), F32))
    hbm, vmem = pl.BlockSpec(memory_space=pltpu.HBM), pl.BlockSpec(memory_space=pltpu.VMEM)
    both = pl.pallas_call(
        tile_kernel,
        out_shape=jax.ShapeDtypeStruct((8, width), F32),
        in_specs=[hbm] * 9,
        out_specs=vmem,
        scratch_shapes=[
            pltpu.VMEM((2 * segments, TILE), F32),
            pltpu.VMEM((width, width), F32),
            pltpu.VMEM((width, width), F32),
            pltpu.VMEM((4, TILE), F32),
            pltpu.VMEM((4, TILE), F32),
            pltpu.VMEM((tiles, TILE, TILE), BF16),
            pltpu.VMEM((tiles, TILE), BF16),
            pltpu.VMEM((tiles, TILE), F32),
            pltpu.VMEM((1, tiles), jnp.int32),
            pltpu.VMEM((1, tiles), jnp.int32),
            pltpu.VMEM((1, tiles), jnp.int32),
            pltpu.VMEM((tiles // 8, 32, TILE), F32),
            pltpu.VMEM((tiles, TILE), F32),
            pltpu.VMEM((tiles, TILE), F32),
            pltpu.VMEM((2 * segments, TILE), F32),
            pltpu.SemaphoreType.DMA((8,)),
            pltpu.SemaphoreType.DMA((PARTS,)),
            *works,
            *boxes,
            *[pltpu.SemaphoreType.DMA((SIZES["y"],))] * 2,
            *[pltpu.SemaphoreType.DMA((len(GROUPS),))] * 4,
            pltpu.VMEM((segments // 2, TILE), F32),
            pltpu.VMEM((segments, TILE), F32),
            pltpu.VMEM((segments, TILE), F32),
            pltpu.VMEM((4, times // 2, TILE), F32),
            pltpu.VMEM((4, times // 2, TILE), F32),
            pltpu.VMEM((times // 2, width, TILE), F32),
            pltpu.VMEM((times // 2, width, TILE), F32),
            pltpu.VMEM((segments, TILE), F32),
            pltpu.VMEM((segments, TILE), F32),
            pltpu.VMEM((segments, TILE), F32),
            pltpu.VMEM((2, width, TILE), F32),
            pltpu.VMEM((2, width, TILE), F32),
        ],
        compiler_params=pltpu.CompilerParams(
            collective_id=0, has_side_effects=True, vmem_limit_bytes=62 << 20
        ),
    )(
        op,
        val,
        wgt,
        step.reshape(1, -1),
        block.reshape(1, -1),
        live.reshape(1, -1),
        transition,
        predicted_precision.reshape(4, TILE),
        starting_mean.reshape(4, TILE),
    )
    return both[:4], both[:4] + both[4:]


def shards(op, val, wgt, step, block, live, transition, predicted_precision, starting_mean):
    segments = 4 * 4 * lax.axis_size("tm")
    return smoother(
        op, val, wgt, step, block, live, transition, predicted_precision, starting_mean, segments
    )


def solution(mesh):
    both = ("tm", "sensor")
    in_specs = (P(both, None, None), P(both, None), P(both, None), P(both), P(both), P(both), P(), P(), P())
    out_specs = (P("tm", None), P("tm", None))
    return jax.shard_map(shards, mesh=mesh, in_specs=in_specs, out_specs=out_specs, check_vma=False)
```
